256 devices in a mesh: half: 2 (over core), member: 16 (over y, x), tile: 8 (over z).
Axes of the slice: x: 4, y: 4, z: 8, core: 2. Of those that a mesh axis runs over, the one named last changes fastest.
Arguments:
- state: float32 [32, 16, 512, 1024], P(('half', 'member'), None, 'tile'), may hold values from -6 to 6
- weights: float32 [32, 512, 1024], P(('half', 'member'), 'tile'), may hold values from -6 to 6
- land_mask: int32 [512, 1024], P('tile'), may hold values 0 or 1
- level_gain: float32 [16], replicated, may hold values from 0.3 to 1
- depth: float32 [16], replicated, may hold values from 0.5 to 2
- obs_row: int32 [131072], P('tile'), may hold values from 1 to 62
- obs_col: int32 [131072], P('tile'), may hold values from 0 to 1023
- obs_quad: int32 [131072], P('tile'), may hold values from 0 to 3
- obs_frac: float32 [2, 131072], P(None, 'tile'), may hold values from 0 to 1
- obs_value: float32 [131072], P('tile'), may hold values from -6 to 6
- obs_error: float32 [131072], P('tile'), may hold values from 0.3 to 3
- noise: float32 [32, 131072], P(('half', 'member'), 'tile'), may hold values from -6 to 6
Outputs:
- stepped: float32 [32, 16, 512, 1024], P(('half', 'member'), None, 'tile')
- new_weights: float32 [32, 512, 1024], P(('half', 'member'), 'tile')
- misfit: float32 [32, 131072], P(None, ('half', 'member', 'tile'))
The draws below stay inside these ranges and needn't reach their ends.
All inputs are finite; a program needn't handle non-finite values. No bound on the sum of `land_mask` on one device may be relied on, other than what follows from the above.
Results may differ from the reference program's by a relative error of at most 0.000071.
Values sent between devices are 32-bit elements; how exact they have to be, the bound alone decides.
No kernel may reach another device: no remote copies, remote signals or barrier semaphores. Data moves between devices by JAX's collectives and lax.ppermute only.
A program may use at most 128 MiB of HBM per device.

```python
import math
import jax
import jax.numpy as jnp
from jax import lax

COLS = 1024
ROWS_DEV = 64
LEVELS = 16
OBS_DEV = 16384
MEMBERS = 32
ROWS = 512
OBS = 131072
OBS_SH = 512
N_TILE = 8


def touch_ends(entries, key, least, high):
    longest = entries.shape.index(max(entries.shape))
    spots = []
    for shift in (0, 1):
        where = [jax.random.randint(jax.random.fold_in(key, axis), (), 0, length) for axis, length in enumerate(entries.shape)]
        where[longest] = (where[longest] + shift) % entries.shape[longest]
        spots.append(tuple(where))
    return entries.at[spots[0]].set(least).at[spots[1]].set(high)


def steps_of(stream_key, shape, shards, smallest, high):
    loudness, own = 1.0, jax.random.fold_in(stream_key, 6)
    for dim, blocks in shards:
        draws = jnp.exp(jax.random.uniform(jax.random.fold_in(own, dim), (blocks,), jnp.float32, smallest / len(shards), high / len(shards)))
        loudness = loudness * jnp.repeat(draws, shape[dim] // blocks).reshape([-1 if axis == dim else 1 for axis in range(len(shape))])
    return loudness


def bell_draw(stream_key, dims, deviation, most, shards=(), kind=jnp.bfloat16):
    drawn = jax.random.normal(stream_key, dims, jnp.float32) * deviation
    if len(shards) > 0:
        drawn = steps_of(stream_key, dims, shards, -0.22, 0.18) * drawn
    return jnp.clip(drawn, min=-most, max=most).astype(kind)


def setup_inputs(seed: int = 0) -> dict:
    key_list = jax.random.split(jax.random.key(seed), 13)
    return {
        "state": bell_draw(key_list[0], (MEMBERS, LEVELS, ROWS, COLS), 1.0, 6.0, ((0, 32), (2, 8)), jnp.float32),
        "weights": bell_draw(key_list[1], (MEMBERS, ROWS, COLS), 1.0, 6.0, ((0, 32), (1, 8)), jnp.float32),
        "land_mask": touch_ends((jax.random.randint(key_list[2], (ROWS, COLS), 0, 4) < 3).astype(jnp.int32), jax.random.fold_in(key_list[2], 1), 0, 1),
        "level_gain": jnp.clip(jnp.exp(jax.random.uniform(key_list[3], (LEVELS,), jnp.float32, math.log(0.3), math.log(1.0))), 0.3, 1.0),
        "depth": jnp.clip(jnp.exp(jax.random.uniform(key_list[4], (LEVELS,), jnp.float32, math.log(0.5), math.log(2.0))), 0.5, 2.0),
        "obs_row": touch_ends(jax.random.randint(key_list[5], (OBS,), 1, ROWS_DEV - 1), jax.random.fold_in(key_list[5], 1), 1, (ROWS_DEV - 1) - 1).astype(jnp.int32),
        "obs_col": touch_ends(jax.random.randint(key_list[6], (OBS,), 0, COLS), jax.random.fold_in(key_list[6], 1), 0, COLS - 1).astype(jnp.int32),
        "obs_quad": touch_ends(jax.random.randint(key_list[7], (OBS,), 0, 4), jax.random.fold_in(key_list[7], 1), 0, 3).astype(jnp.int32),
        "obs_frac": jnp.clip(1.0 * jax.random.uniform(key_list[8], (2, OBS), jnp.float32) ** steps_of(key_list[8], (2, OBS), ((1, 8),), -0.2, 0.2), 0.0, 1.0),
        "obs_value": bell_draw(key_list[9], (OBS,), 1.0, 6.0, ((0, 8),), jnp.float32),
        "obs_error": jnp.clip(jnp.exp(math.log(3.0) - 2.3025851 * jax.random.uniform(key_list[10], (OBS,), jnp.float32) ** steps_of(key_list[10], (OBS,), ((0, 8),), -0.2, 0.2)), 0.3, 3.0),
        "noise": bell_draw(key_list[11], (MEMBERS, OBS), 1.0, 6.0, ((0, 32), (1, 8)), jnp.float32),
    }


def laplace_step(state_one, weight_one, land_mask, level_gain):
    diffusivity = 0.24 * jax.nn.sigmoid(weight_one)
    ocean_cells = land_mask.astype(jnp.float32)
    zero_row = jnp.zeros_like(state_one[:, :1])
    upper = jnp.concatenate([zero_row, state_one[:, :-1]], axis=1)
    lower = jnp.concatenate([state_one[:, 1:], zero_row], axis=1)
    laplacian = upper + lower + jnp.roll(state_one, 1, axis=2) + jnp.roll(state_one, -1, axis=2) - 4.0 * state_one
    return state_one + level_gain[:, None, None] * (ocean_cells * diffusivity)[None] * laplacian

def interpolate(column, row_index, col_index, obs_quad, obs_frac):
    width = column.shape[1]
    row_step = jnp.where(obs_quad % 2 == 1, 1, -1).astype(jnp.int32)
    col_step = jnp.where(obs_quad // 2 == 1, 1, -1).astype(jnp.int32)
    row_other = (row_index + row_step).astype(jnp.int32)
    col_other = ((col_index + col_step) % width).astype(jnp.int32)
    flat = column.reshape(-1)
    corner_aa = jnp.take(flat, row_index * width + col_index)
    corner_ab = jnp.take(flat, row_index * width + col_other)
    corner_ba = jnp.take(flat, row_other * width + col_index)
    corner_bb = jnp.take(flat, row_other * width + col_other)
    first = obs_frac[0]
    second = obs_frac[1]
    return (1.0 - first) * (1.0 - second) * corner_aa + (1.0 - first) * second * corner_ab + first * (1.0 - second) * corner_ba + first * second * corner_bb

def reference(state, weights, land_mask, level_gain, depth, obs_row, obs_col, obs_quad, obs_frac, obs_value, obs_error, noise):
    highest = lax.Precision.HIGHEST
    tile_of = (jnp.arange(OBS) // OBS_DEV).astype(jnp.int32)
    global_row = (obs_row + tile_of * ROWS_DEV).astype(jnp.int32)

    def member_step(pair):
        state_one, weight_one = pair
        stepped_one = laplace_step(state_one, weight_one, land_mask, level_gain)
        column = lax.optimization_barrier(jnp.sum(depth[:, None, None] * stepped_one, axis=0)) / math.sqrt(LEVELS)
        return (stepped_one, interpolate(column, global_row, obs_col, obs_quad, obs_frac))
    stepped, predictions = lax.map(member_step, (state, weights))
    residual = obs_value[None] + noise - predictions
    anomaly = predictions - lax.optimization_barrier(jnp.mean(predictions, axis=0, keepdims=True))
    weighted = anomaly / obs_error[None]
    gram = jnp.einsum('ko,jo->kj', weighted, anomaly, precision=highest)
    products = jnp.einsum('ko,jo->kj', weighted, residual, precision=highest)
    identity = jnp.eye(MEMBERS, dtype=jnp.float32)
    factor = jnp.linalg.cholesky(identity + gram / OBS)
    coefficients = jax.scipy.linalg.cho_solve((factor, True), products / OBS)
    combination = identity + coefficients - lax.optimization_barrier(jnp.mean(coefficients, axis=0, keepdims=True))
    new_weights = jnp.einsum('kj,krc->jrc', combination, weights, precision=highest)
    misfit = residual.reshape(MEMBERS, N_TILE, MEMBERS, OBS_SH).transpose(0, 2, 1, 3).reshape(MEMBERS, OBS)
    return (stepped, new_weights, misfit)
```

```python
import math

import jax
import jax.numpy as jnp
from jax import lax
from jax.experimental import pallas as pl
from jax.experimental.pallas import tpu as pltpu
from jax.sharding import PartitionSpec as P

LANES = 128
SUBLANES = 8
LEVELS_STEP = 2


def step_and_sample(
    gain_ref,
    depth_ref,
    state_ref,
    low_ref,
    high_ref,
    weights_ref,
    land_ref,
    row_ref,
    col_ref,
    quad_ref,
    frac_ref,
    perturbed_ref,
    stepped_ref,
    predicted_ref,
    residual_ref,
    diffusivity_ref,
    column_ref,
    even_ref,
    odd_ref,
):
    step = pl.program_id(0)
    steps = pl.num_programs(0)
    levels, rows, cols = state_ref.shape
    sub = lax.broadcasted_iota(jnp.int32, (SUBLANES, cols), 0)

    @pl.when(step == 0)
    def _():
        diffusivity_ref[...] = land_ref[...].astype(jnp.float32) * (
            0.24 * jax.nn.sigmoid(weights_ref[...])
        )
        column_ref[...] = jnp.zeros_like(column_ref)

    for start in range(0, rows, SUBLANES):
        here = pl.ds(start, SUBLANES)
        total = column_ref[here, :]
        diffusivity = diffusivity_ref[here, :]
        for level in range(levels):
            centre = state_ref[level, here, :]
            if start == 0:
                above_row = low_ref[level]
            else:
                above_row = state_ref[level, pl.ds(start - 1, 1), :]
            if start + SUBLANES == rows:
                below_row = high_ref[level]
            else:
                below_row = state_ref[level, pl.ds(start + SUBLANES, 1), :]
            above = jnp.where(sub == 0, above_row, pltpu.roll(centre, 1, 0))
            below = jnp.where(
                sub == SUBLANES - 1, below_row, pltpu.roll(centre, SUBLANES - 1, 0)
            )
            laplacian = (
                above
                + below
                + pltpu.roll(centre, 1, 1)
                + pltpu.roll(centre, cols - 1, 1)
                - 4.0 * centre
            )
            number = step * levels + level
            stepped = centre + gain_ref[number] * diffusivity * laplacian
            stepped_ref[level, here, :] = stepped
            total = total + depth_ref[number] * stepped
        column_ref[here, :] = total

    @pl.when(step == steps - 1)
    def _():
        scale = 1.0 / math.sqrt(levels * steps)
        lane = lax.broadcasted_iota(jnp.int32, (SUBLANES, LANES), 1)
        doubled = (2 * lane) % LANES
        first_half = lane < LANES // 2

        def pick(table, index):
            return jnp.take_along_axis(table, index, axis=1, mode="promise_in_bounds")

        for start in range(0, rows, SUBLANES):
            here = pl.ds(start, SUBLANES)
            for part in range(cols // (2 * LANES)):
                left = column_ref[here, pl.ds(2 * part * LANES, LANES)] * scale
                right = column_ref[here, pl.ds((2 * part + 1) * LANES, LANES)] * scale
                out = pl.ds(part * LANES, LANES)
                even_ref[here, out] = jnp.where(
                    first_half, pick(left, doubled), pick(right, doubled)
                )
                odd_ref[here, out] = jnp.where(
                    first_half, pick(left, doubled + 1), pick(right, doubled + 1)
                )

        sub_here = lax.broadcasted_iota(jnp.int32, (SUBLANES, LANES), 0)

        def sample(i, carry):
            def spread(value):
                return jnp.broadcast_to(value, (SUBLANES, LANES))

            one = pl.ds(i, 1)
            row = spread(row_ref[one, :])
            col = spread(col_ref[one, :])
            quad = spread(quad_ref[one, :])
            place = pl.ds(pl.multiple_of(i * LANES, LANES), LANES)
            first = spread(frac_ref[pl.ds(0, 1), place])
            second = spread(frac_ref[pl.ds(1, 1), place])
            row_other = row + jnp.where((quad & 1) == 1, 1, -1)
            col_other = (col + jnp.where((quad >> 1) == 1, 1, -1)) & (cols - 1)
            is_even = (col & 1) == 0
            even_at = jnp.where(is_even, col, col_other) >> 1
            odd_at = jnp.where(is_even, col_other, col) >> 1
            even_by = jnp.where(is_even, 1.0 - second, second)
            odd_by = jnp.where(is_even, second, 1.0 - second)
            even_lane, even_part = even_at & (LANES - 1), even_at // LANES
            odd_lane, odd_part = odd_at & (LANES - 1), odd_at // LANES
            parts = cols // (2 * LANES)
            even_here = [even_part == part for part in range(1, parts)]
            odd_here = [odd_part == part for part in range(1, parts)]
            total = jnp.zeros((SUBLANES, LANES), jnp.float32)
            for start in range(0, rows, SUBLANES):
                here = pl.ds(start, SUBLANES)
                even = pick(even_ref[here, pl.ds(0, LANES)], even_lane)
                odd = pick(odd_ref[here, pl.ds(0, LANES)], odd_lane)
                for part in range(1, parts):
                    out = pl.ds(part * LANES, LANES)
                    even = jnp.where(
                        even_here[part - 1], pick(even_ref[here, out], even_lane), even
                    )
                    odd = jnp.where(
                        odd_here[part - 1], pick(odd_ref[here, out], odd_lane), odd
                    )
                by_row = jnp.where(
                    sub_here == row - start,
                    1.0 - first,
                    jnp.where(sub_here == row_other - start, first, 0.0),
                )
                total = total + by_row * (even_by * even + odd_by * odd)
            predicted_ref[one, :] = jnp.sum(total, axis=0, keepdims=True)
            return carry

        lax.fori_loop(0, row_ref.shape[0], sample, 0, unroll=2)
        residual_ref[...] = perturbed_ref[...] - predicted_ref[...]


def forward(
    level_gain, depth, state, low, high, weights, land_mask, row, col, quad, frac, perturbed
):
    levels, rows, cols = state.shape
    per = LEVELS_STEP

    def whole(array):
        return pl.BlockSpec(array.shape, lambda i: (0,) * array.ndim)

    smem = pl.BlockSpec(memory_space=pltpu.SMEM)
    halo = pl.BlockSpec((per, 1, cols), lambda i: (i, 0, 0))
    field = pl.BlockSpec((per, rows, cols), lambda i: (i, 0, 0))
    return pl.pallas_call(
        step_and_sample,
        grid=(levels // per,),
        in_specs=[smem, smem, field, halo, halo]
        + [whole(array) for array in (weights, land_mask, row, col, quad, frac, perturbed)],
        out_specs=[field, whole(row), whole(row)],
        out_shape=[
            jax.ShapeDtypeStruct(state.shape, jnp.float32),
            jax.ShapeDtypeStruct(row.shape, jnp.float32),
            jax.ShapeDtypeStruct(row.shape, jnp.float32),
        ],
        scratch_shapes=[
            pltpu.VMEM((rows, cols), jnp.float32),
            pltpu.VMEM((rows, cols), jnp.float32),
            pltpu.VMEM((rows, cols // 2), jnp.float32),
            pltpu.VMEM((rows, cols // 2), jnp.float32),
        ],
        compiler_params=pltpu.CompilerParams(vmem_limit_bytes=24 * 1024 * 1024),
        name="step_and_sample",
    )(level_gain, depth, state, low, high, weights, land_mask, row, col, quad, frac, perturbed)


def on_device(
    state,
    weights,
    land_mask,
    level_gain,
    depth,
    obs_row,
    obs_col,
    obs_quad,
    obs_frac,
    obs_value,
    obs_error,
    noise,
):
    highest = lax.Precision.HIGHEST
    axes = ("half", "member")
    members = lax.axis_size(axes)
    member_index = lax.axis_index(axes)
    tile_count = lax.axis_size("tile")
    obs_local = obs_row.shape[0]
    shard_size = obs_local // members
    total_obs = obs_local * tile_count
    own = state[0]
    up = [(i, i + 1) for i in range(tile_count - 1)]
    down = [(target, source) for source, target in up]
    low = lax.ppermute(own[:, -1:], "tile", up)
    high = lax.ppermute(own[:, :1], "tile", down)
    grid = (obs_local // LANES, LANES)
    perturbed = (obs_value + noise[0]).reshape(grid)
    stepped, predicted, residual = forward(
        level_gain,
        depth,
        own,
        low,
        high,
        weights[0],
        land_mask,
        obs_row.reshape(grid),
        obs_col.reshape(grid),
        obs_quad.reshape(grid),
        obs_frac,
        perturbed,
    )
    grouped = lax.all_to_all(
        predicted.reshape(members, shard_size), axes, split_axis=0, concat_axis=0, tiled=True
    )
    misfit = lax.all_to_all(
        residual.reshape(members, shard_size), axes, split_axis=0, concat_axis=0, tiled=True
    )
    error_shard = lax.dynamic_slice_in_dim(obs_error, member_index * shard_size, shard_size, 0)
    anomaly = grouped - jnp.mean(grouped, axis=0, keepdims=True)
    weighted = anomaly / error_shard[None]
    gram = jnp.einsum("ko,jo->kj", weighted, anomaly, precision=highest)
    products = jnp.einsum("ko,jo->kj", weighted, misfit, precision=highest)
    gram, products = lax.psum((gram, products), ("half", "member", "tile"))
    identity = jnp.eye(members, dtype=jnp.float32)
    factor = jnp.linalg.cholesky(identity + gram / total_obs)
    coefficients = jax.scipy.linalg.cho_solve((factor, True), products / total_obs)
    combination = identity + coefficients - jnp.mean(coefficients, axis=0, keepdims=True)
    own_column = lax.dynamic_slice_in_dim(combination, member_index, 1, 1)[:, 0]
    new_weights = jnp.einsum(
        "k,krc->rc",
        own_column,
        lax.all_gather(weights, axes, axis=0, tiled=True),
        precision=highest,
    )[None]
    return (stepped[None], new_weights, misfit)


def solution(mesh):
    in_specs = (
        P(("half", "member"), None, "tile", None),
        P(("half", "member"), "tile", None),
        P("tile", None),
        P(),
        P(),
        P("tile"),
        P("tile"),
        P("tile"),
        P(None, "tile"),
        P("tile"),
        P("tile"),
        P(("half", "member"), "tile"),
    )
    out_specs = (
        P(("half", "member"), None, "tile", None),
        P(("half", "member"), "tile", None),
        P(None, ("half", "member", "tile")),
    )
    return jax.shard_map(
        on_device, mesh=mesh, in_specs=in_specs, out_specs=out_specs, check_vma=False
    )
```

```python
import functools
import math

import jax
import jax.numpy as jnp
from jax import lax
from jax.experimental import pallas as pl
from jax.experimental.pallas import tpu as pltpu
from jax.sharding import PartitionSpec as P

LANES = 128
SUBLANES = 8
LEVELS_STEP = 8
OBS_STEP = 2048
KEYS = 256
VMEM_BYTES = 60 * 1024 * 1024


def pick(table, index):
    return jnp.take_along_axis(table, index, axis=1, mode="promise_in_bounds")


def step_and_sample(
    gain_ref,
    depth_ref,
    state_ref,
    low_ref,
    high_ref,
    weights_ref,
    land_ref,
    row_ref,
    col_ref,
    quad_ref,
    frac_ref,
    value_ref,
    noise_ref,
    stepped_ref,
    sampled_ref,
    diffusivity_ref,
    column_ref,
    even_ref,
    odd_ref,
):
    step = pl.program_id(0)
    steps = pl.num_programs(0)
    levels, rows, cols = state_ref.shape
    sub = lax.broadcasted_iota(jnp.int32, (SUBLANES, cols), 0)

    @pl.when(step == 0)
    def _():
        diffusivity_ref[...] = land_ref[...].astype(jnp.float32) * (
            0.24 * jax.nn.sigmoid(weights_ref[...])
        )
        column_ref[...] = jnp.zeros_like(column_ref)

    for start in range(0, rows, SUBLANES):
        here = pl.ds(start, SUBLANES)
        total = column_ref[here, :]
        diffusivity = diffusivity_ref[here, :]
        for level in range(levels):
            centre = state_ref[level, here, :]
            if start == 0:
                above_row = low_ref[level]
            else:
                above_row = state_ref[level, pl.ds(start - 1, 1), :]
            if start + SUBLANES == rows:
                below_row = high_ref[level]
            else:
                below_row = state_ref[level, pl.ds(start + SUBLANES, 1), :]
            above = jnp.where(sub == 0, above_row, pltpu.roll(centre, 1, 0))
            below = jnp.where(
                sub == SUBLANES - 1, below_row, pltpu.roll(centre, SUBLANES - 1, 0)
            )
            laplacian = (
                above
                + below
                + pltpu.roll(centre, 1, 1)
                + pltpu.roll(centre, cols - 1, 1)
                - 4.0 * centre
            )
            number = step * levels + level
            stepped = centre + gain_ref[number] * diffusivity * laplacian
            stepped_ref[level, here, :] = stepped
            total = total + depth_ref[number] * stepped
        column_ref[here, :] = total

    @pl.when(step == steps - 1)
    def _():
        scale = 1.0 / math.sqrt(levels * steps)
        lane = lax.broadcasted_iota(jnp.int32, (SUBLANES, LANES), 1)
        doubled = (2 * lane) % LANES
        first_half = lane < LANES // 2
        for block in range(cols // (2 * LANES)):
            evens, odds = [], []
            for start in range(0, rows, SUBLANES):
                here = pl.ds(start, SUBLANES)
                left = column_ref[here, pl.ds(2 * block * LANES, LANES)] * scale
                right = column_ref[here, pl.ds((2 * block + 1) * LANES, LANES)] * scale
                evens.append(jnp.where(first_half, pick(left, doubled), pick(right, doubled)))
                odds.append(
                    jnp.where(first_half, pick(left, doubled + 1), pick(right, doubled + 1))
                )
            part, key = divmod(block * LANES, KEYS)
            for ref, pieces in ((even_ref, evens), (odd_ref, odds)):
                table = jnp.concatenate(pieces, axis=0)
                coarse = table.astype(jnp.bfloat16)
                fine = (table - coarse.astype(jnp.float32)).astype(jnp.bfloat16)
                ref[pl.ds(2 * part * rows, rows), pl.ds(key, LANES)] = coarse
                ref[pl.ds((2 * part + 1) * rows, rows), pl.ds(key, LANES)] = fine

        count = OBS_STEP // LANES
        keys = lax.broadcasted_iota(jnp.int32, (KEYS, OBS_STEP), 0)
        grid_row = lax.broadcasted_iota(jnp.int32, (rows, OBS_STEP), 0)
        shard_rows = SUBLANES // 2

        def look_up(ref, at):
            chosen = jnp.where(keys == (at & (KEYS - 1)), 1.0, 0.0).astype(jnp.bfloat16)
            found = jnp.dot(ref[...], chosen, preferred_element_type=jnp.float32)
            result = found[:rows] + found[rows : 2 * rows]
            for part in range(1, cols // (2 * KEYS)):
                base = 2 * part * rows
                other = found[base : base + rows] + found[base + rows : base + 2 * rows]
                result = jnp.where(at // KEYS == part, other, result)
            return result

        def sample(i, carry):
            def line(ref):
                return jnp.concatenate(
                    [ref[pl.ds(i * count + q, 1), :] for q in range(count)], axis=1
                )

            row, col, quad = line(row_ref), line(col_ref), line(quad_ref)
            place = pl.ds(pl.multiple_of(i * OBS_STEP, OBS_STEP), OBS_STEP)
            first = frac_ref[pl.ds(0, 1), place]
            second = frac_ref[pl.ds(1, 1), place]
            row_other = row + jnp.where((quad & 1) == 1, 1, -1)
            col_other = (col + jnp.where((quad >> 1) == 1, 1, -1)) & (cols - 1)
            is_even = (col & 1) == 0
            even_at = jnp.where(is_even, col, col_other) >> 1
            odd_at = jnp.where(is_even, col_other, col) >> 1
            even_by = jnp.where(is_even, 1.0 - second, second)
            odd_by = jnp.where(is_even, second, 1.0 - second)
            along = even_by * look_up(even_ref, even_at) + odd_by * look_up(odd_ref, odd_at)
            by_row = jnp.where(
                grid_row == row, 1.0 - first, jnp.where(grid_row == row_other, first, 0.0)
            )
            predicted = jnp.sum(by_row * along, axis=0, keepdims=True)
            residual = line(value_ref) + line(noise_ref) - predicted
            for q in range(count):
                shard, inner = divmod(q, shard_rows)
                to = (i * (count // shard_rows) + shard) * SUBLANES + inner
                lanes = slice(q * LANES, (q + 1) * LANES)
                sampled_ref[pl.ds(to, 1), :] = predicted[:, lanes]
                sampled_ref[pl.ds(to + shard_rows, 1), :] = residual[:, lanes]
            return carry

        lax.fori_loop(0, row_ref.shape[0] // count, sample, 0)


def forward(level_gain, depth, state, low, high, weights, land_mask, obs):
    levels, rows, cols = state.shape
    per = LEVELS_STEP
    members_rows = 2 * obs[0].shape[0]

    def whole(shape):
        return pl.BlockSpec(shape, lambda i: (0,) * len(shape))

    smem = pl.BlockSpec(memory_space=pltpu.SMEM)
    halo = pl.BlockSpec((per, 1, cols), lambda i: (i, 0, 0))
    field = pl.BlockSpec((per, rows, cols), lambda i: (i, 0, 0))
    table = pltpu.VMEM((2 * rows * cols // (2 * KEYS), KEYS), jnp.bfloat16)
    return pl.pallas_call(
        step_and_sample,
        grid=(levels // per,),
        in_specs=[smem, smem, field, halo, halo]
        + [whole(array.shape) for array in (weights, land_mask, *obs)],
        out_specs=[field, whole((members_rows, LANES))],
        out_shape=[
            jax.ShapeDtypeStruct(state.shape, jnp.float32),
            jax.ShapeDtypeStruct((members_rows, LANES), jnp.float32),
        ],
        scratch_shapes=[
            pltpu.VMEM((rows, cols), jnp.float32),
            pltpu.VMEM((rows, cols), jnp.float32),
            table,
            table,
        ],
        compiler_params=pltpu.CompilerParams(vmem_limit_bytes=VMEM_BYTES),
        name="step_and_sample",
    )(level_gain, depth, state, low, high, weights, land_mask, *obs)


def shard_products(index_ref, grouped_ref, error_ref, misfit_ref, products_ref):
    members = misfit_ref.shape[0]
    half_rows = SUBLANES // 2

    def lines(first):
        return jnp.concatenate(
            [grouped_ref[pl.ds(first + q, members, stride=SUBLANES), :] for q in range(half_rows)],
            axis=1,
        )

    grouped, misfit = lines(0), lines(half_rows)
    misfit_ref[...] = misfit
    error = jnp.concatenate(
        [error_ref[pl.ds(index_ref[0] * half_rows + q, 1), :] for q in range(half_rows)], axis=1
    )
    anomaly = grouped - jnp.sum(grouped, axis=0, keepdims=True) * (1.0 / members)
    weighted = anomaly / error
    blank = jnp.zeros((LANES - 2 * members, grouped.shape[1]), jnp.float32)
    products_ref[...] = lax.dot_general(
        weighted,
        jnp.concatenate([anomaly, misfit, blank], axis=0),
        (((1,), (1,)), ((), ())),
        precision=lax.Precision.HIGHEST,
        preferred_element_type=jnp.float32,
    )


def solve_and_combine(
    total_obs, index_ref, *refs
):
    *product_refs, weights_ref, out_ref, held_ref, by_ref, sems = refs
    members, rows, _ = weights_ref.shape
    parts = sems.shape[0]
    part_rows = rows // parts

    def copy(part):
        here = pl.ds(part * part_rows, part_rows)
        return pltpu.make_async_copy(
            weights_ref.at[:, here, :], held_ref.at[:, here, :], sems.at[part]
        )

    for part in range(parts):
        copy(part).start()

    row = lax.broadcasted_iota(jnp.int32, (members, LANES), 0)
    lane = lax.broadcasted_iota(jnp.int32, (members, LANES), 1)
    system = product_refs[0][...]
    for ref in product_refs[1:]:
        system = system + ref[...]
    system = system / total_obs + jnp.where(row == lane, 1.0, 0.0)
    for k in range(members):
        pivot_row = system[k : k + 1, :] * (1.0 / system[k : k + 1, k : k + 1])
        system = jnp.where(row == k, pivot_row, system - system[:, k : k + 1] * pivot_row)
    index = index_ref[0]
    own = jnp.sum(
        jnp.where(lane == members + index, system, 0.0), axis=1, keepdims=True
    )
    own = own - jnp.sum(own, axis=0, keepdims=True) * (1.0 / members)
    by_ref[...] = jnp.where(row == index, 1.0, 0.0) + own

    for part in range(parts):
        copy(part).wait()
        for start in range(part * part_rows, (part + 1) * part_rows, SUBLANES):
            here = pl.ds(start, SUBLANES)
            total = jnp.zeros((SUBLANES, weights_ref.shape[2]), jnp.float32)
            for k in range(members):
                total = total + by_ref[pl.ds(k, 1), pl.ds(0, 1)] * held_ref[k, here, :]
            out_ref[here, :] = total


def combine(total_obs, index, products, weights):
    members, rows, cols = weights.shape
    parts = 4
    vmem = pl.BlockSpec(memory_space=pltpu.VMEM)
    return pl.pallas_call(
        functools.partial(solve_and_combine, total_obs),
        in_specs=[pl.BlockSpec(memory_space=pltpu.SMEM)]
        + [vmem] * len(products)
        + [pl.BlockSpec(memory_space=pl.ANY)],
        out_specs=vmem,
        out_shape=jax.ShapeDtypeStruct((rows, cols), jnp.float32),
        scratch_shapes=[
            pltpu.VMEM((members, rows, cols), jnp.float32),
            pltpu.VMEM((members, LANES), jnp.float32),
            pltpu.SemaphoreType.DMA((parts,)),
        ],
        compiler_params=pltpu.CompilerParams(vmem_limit_bytes=VMEM_BYTES),
        name="solve_and_combine",
    )(index, *products, weights)


def exchange(array, axis, moves):
    return [array] + [lax.ppermute(array, axis, list(enumerate(move))) for move in moves]


def on_device(
    state,
    weights,
    land_mask,
    level_gain,
    depth,
    obs_row,
    obs_col,
    obs_quad,
    obs_frac,
    obs_value,
    obs_error,
    noise,
):
    axes = ("half", "member")
    members = lax.axis_size(axes)
    index = lax.axis_index(axes).astype(jnp.int32).reshape(1)
    chips = lax.axis_size("member")
    side = math.isqrt(chips)
    tile_count = lax.axis_size("tile")
    obs_local = obs_row.shape[0]
    total_obs = obs_local * tile_count
    own = state[0]
    up = [(i, i + 1) for i in range(tile_count - 1)]
    down = [(target, source) for source, target in up]
    low = lax.ppermute(own[:, -1:], "tile", up)
    high = lax.ppermute(own[:, :1], "tile", down)
    grid = (obs_local // LANES, LANES)
    obs = (
        obs_row.reshape(grid),
        obs_col.reshape(grid),
        obs_quad.reshape(grid),
        obs_frac,
        obs_value.reshape(grid),
        noise.reshape(grid),
    )
    gathered = lax.all_gather(weights, axes, axis=0, tiled=True)
    stepped, sampled = forward(level_gain, depth, own, low, high, weights[0], land_mask, obs)
    grouped = lax.all_to_all(
        sampled.reshape(members, SUBLANES, LANES), axes, split_axis=0, concat_axis=0, tiled=True
    )
    vmem = pl.BlockSpec(memory_space=pltpu.VMEM)
    misfit, products = pl.pallas_call(
        shard_products,
        in_specs=[pl.BlockSpec(memory_space=pltpu.SMEM), vmem, vmem],
        out_specs=[vmem, vmem],
        out_shape=[
            jax.ShapeDtypeStruct((members, obs_local // members), jnp.float32),
            jax.ShapeDtypeStruct((members, LANES), jnp.float32),
        ],
        compiler_params=pltpu.CompilerParams(vmem_limit_bytes=VMEM_BYTES),
        name="shard_products",
    )(index, grouped.reshape(members * SUBLANES, LANES), obs_error.reshape(grid))

    def along_x(shift):
        return [(m // side) * side + (m % side + shift) % side for m in range(chips)]

    def along_y(shift):
        return [(m + shift * side) % chips for m in range(chips)]

    def along_z(shift):
        return [(t + shift) % tile_count for t in range(tile_count)]

    products = sum(exchange(products, "half", [(1, 0)]))
    products = sum(exchange(products, "member", [along_x(s) for s in (1, 3, 2)]))
    products = sum(exchange(products, "member", [along_y(s) for s in (1, 3, 2)]))
    products = sum(exchange(products, "tile", [along_z(1)]))
    products = exchange(products, "tile", [along_z(s) for s in (2, 6, 4)])
    new_weights = combine(total_obs, index, products, gathered)
    return (stepped[None], new_weights[None], misfit)


def solution(mesh):
    in_specs = (
        P(("half", "member"), None, "tile", None),
        P(("half", "member"), "tile", None),
        P("tile", None),
        P(),
        P(),
        P("tile"),
        P("tile"),
        P("tile"),
        P(None, "tile"),
        P("tile"),
        P("tile"),
        P(("half", "member"), "tile"),
    )
    out_specs = (
        P(("half", "member"), None, "tile", None),
        P(("half", "member"), "tile", None),
        P(None, ("half", "member", "tile")),
    )
    return jax.shard_map(
        on_device, mesh=mesh, in_specs=in_specs, out_specs=out_specs, check_vma=False
    )
```

```python
import functools
import math

import jax
import jax.numpy as jnp
from jax import lax
from jax.experimental import pallas as pl
from jax.experimental.pallas import tpu as pltpu
from jax.sharding import PartitionSpec as P

LANES = 128
SUBLANES = 8
LEVELS_STEP = 8
OBS_STEP = 2048
KEYS = 256
PACK_ROWS = 3 * SUBLANES
VMEM_BYTES = 60 * 1024 * 1024
SMALL_VMEM_BYTES = 8 * 1024 * 1024


def pick(table, index):
    return jnp.take_along_axis(table, index, axis=1, mode="promise_in_bounds")


def step_and_sample(
    gain_ref,
    depth_ref,
    state_ref,
    low_ref,
    high_ref,
    weights_ref,
    land_ref,
    row_ref,
    col_ref,
    quad_ref,
    frac_ref,
    value_ref,
    noise_ref,
    stepped_ref,
    sampled_ref,
    diffusivity_ref,
    column_ref,
    even_ref,
    odd_ref,
):
    step = pl.program_id(0)
    steps = pl.num_programs(0)
    levels, rows, cols = state_ref.shape
    sub = lax.broadcasted_iota(jnp.int32, (SUBLANES, cols), 0)

    @pl.when(step == 0)
    def _():
        diffusivity_ref[...] = land_ref[...].astype(jnp.float32) * (
            0.24 * jax.nn.sigmoid(weights_ref[...])
        )
        column_ref[...] = jnp.zeros_like(column_ref)
        for tile in range(rows * cols // (SUBLANES * LANES)):
            at_row, at_col = divmod(tile * LANES, cols)
            to = (tile // 2) * PACK_ROWS + (1 + tile % 2) * SUBLANES
            sampled_ref[pl.ds(to, SUBLANES), :] = weights_ref[
                pl.ds(at_row * SUBLANES, SUBLANES), pl.ds(at_col, LANES)
            ]

    for start in range(0, rows, SUBLANES):
        here = pl.ds(start, SUBLANES)
        total = column_ref[here, :]
        diffusivity = diffusivity_ref[here, :]
        for level in range(levels):
            centre = state_ref[level, here, :]
            if start == 0:
                above_row = low_ref[level]
            else:
                above_row = state_ref[level, pl.ds(start - 1, 1), :]
            if start + SUBLANES == rows:
                below_row = high_ref[level]
            else:
                below_row = state_ref[level, pl.ds(start + SUBLANES, 1), :]
            above = jnp.where(sub == 0, above_row, pltpu.roll(centre, 1, 0))
            below = jnp.where(
                sub == SUBLANES - 1, below_row, pltpu.roll(centre, SUBLANES - 1, 0)
            )
            laplacian = (
                above
                + below
                + pltpu.roll(centre, 1, 1)
                + pltpu.roll(centre, cols - 1, 1)
                - 4.0 * centre
            )
            number = step * levels + level
            stepped = centre + gain_ref[number] * diffusivity * laplacian
            stepped_ref[level, here, :] = stepped
            total = total + depth_ref[number] * stepped
        column_ref[here, :] = total

    @pl.when(step == steps - 1)
    def _():
        scale = 1.0 / math.sqrt(levels * steps)
        lane = lax.broadcasted_iota(jnp.int32, (SUBLANES, LANES), 1)
        doubled = (2 * lane) % LANES
        first_half = lane < LANES // 2
        for block in range(cols // (2 * LANES)):
            evens, odds = [], []
            for start in range(0, rows, SUBLANES):
                here = pl.ds(start, SUBLANES)
                left = column_ref[here, pl.ds(2 * block * LANES, LANES)] * scale
                right = column_ref[here, pl.ds((2 * block + 1) * LANES, LANES)] * scale
                evens.append(jnp.where(first_half, pick(left, doubled), pick(right, doubled)))
                odds.append(
                    jnp.where(first_half, pick(left, doubled + 1), pick(right, doubled + 1))
                )
            part, key = divmod(block * LANES, KEYS)
            for ref, pieces in ((even_ref, evens), (odd_ref, odds)):
                table = jnp.concatenate(pieces, axis=0)
                coarse = table.astype(jnp.bfloat16)
                fine = (table - coarse.astype(jnp.float32)).astype(jnp.bfloat16)
                ref[pl.ds(2 * part * rows, rows), pl.ds(key, LANES)] = coarse
                ref[pl.ds((2 * part + 1) * rows, rows), pl.ds(key, LANES)] = fine

        count = OBS_STEP // LANES
        keys = lax.broadcasted_iota(jnp.int32, (KEYS, OBS_STEP), 0)
        grid_row = lax.broadcasted_iota(jnp.int32, (rows, OBS_STEP), 0)
        shard_rows = SUBLANES // 2

        def look_up(ref, at):
            chosen = jnp.where(keys == (at & (KEYS - 1)), 1.0, 0.0).astype(jnp.bfloat16)
            found = jnp.dot(ref[...], chosen, preferred_element_type=jnp.float32)
            result = found[:rows] + found[rows : 2 * rows]
            for part in range(1, cols // (2 * KEYS)):
                base = 2 * part * rows
                other = found[base : base + rows] + found[base + rows : base + 2 * rows]
                result = jnp.where(at // KEYS == part, other, result)
            return result

        def sample(i, carry):
            def line(ref):
                return jnp.concatenate(
                    [ref[pl.ds(i * count + q, 1), :] for q in range(count)], axis=1
                )

            row, col, quad = line(row_ref), line(col_ref), line(quad_ref)
            place = pl.ds(pl.multiple_of(i * OBS_STEP, OBS_STEP), OBS_STEP)
            first = frac_ref[pl.ds(0, 1), place]
            second = frac_ref[pl.ds(1, 1), place]
            row_other = row + jnp.where((quad & 1) == 1, 1, -1)
            col_other = (col + jnp.where((quad >> 1) == 1, 1, -1)) & (cols - 1)
            is_even = (col & 1) == 0
            even_at = jnp.where(is_even, col, col_other) >> 1
            odd_at = jnp.where(is_even, col_other, col) >> 1
            even_by = jnp.where(is_even, 1.0 - second, second)
            odd_by = jnp.where(is_even, second, 1.0 - second)
            along = even_by * look_up(even_ref, even_at) + odd_by * look_up(odd_ref, odd_at)
            by_row = jnp.where(
                grid_row == row, 1.0 - first, jnp.where(grid_row == row_other, first, 0.0)
            )
            predicted = jnp.sum(by_row * along, axis=0, keepdims=True)
            residual = line(value_ref) + line(noise_ref) - predicted
            for q in range(count):
                shard, inner = divmod(q, shard_rows)
                to = (i * (count // shard_rows) + shard) * PACK_ROWS + inner
                lanes = slice(q * LANES, (q + 1) * LANES)
                sampled_ref[pl.ds(to, 1), :] = predicted[:, lanes]
                sampled_ref[pl.ds(to + shard_rows, 1), :] = residual[:, lanes]
            return carry

        lax.fori_loop(0, row_ref.shape[0] // count, sample, 0)


def forward(level_gain, depth, state, low, high, weights, land_mask, obs):
    levels, rows, cols = state.shape
    per = LEVELS_STEP
    packed = (obs[0].shape[0] // (SUBLANES // 2) * PACK_ROWS, LANES)

    def whole(shape):
        return pl.BlockSpec(shape, lambda i: (0,) * len(shape))

    smem = pl.BlockSpec(memory_space=pltpu.SMEM)
    halo = pl.BlockSpec((per, 1, cols), lambda i: (i, 0, 0))
    field = pl.BlockSpec((per, rows, cols), lambda i: (i, 0, 0))
    table = pltpu.VMEM((2 * rows * cols // (2 * KEYS), KEYS), jnp.bfloat16)
    return pl.pallas_call(
        step_and_sample,
        grid=(levels // per,),
        in_specs=[smem, smem, field, halo, halo]
        + [whole(array.shape) for array in (weights, land_mask, *obs)],
        out_specs=[field, whole(packed)],
        out_shape=[
            jax.ShapeDtypeStruct(state.shape, jnp.float32),
            jax.ShapeDtypeStruct(packed, jnp.float32),
        ],
        scratch_shapes=[
            pltpu.VMEM((rows, cols), jnp.float32),
            pltpu.VMEM((rows, cols), jnp.float32),
            table,
            table,
        ],
        compiler_params=pltpu.CompilerParams(vmem_limit_bytes=VMEM_BYTES),
        name="step_and_sample",
    )(level_gain, depth, state, low, high, weights, land_mask, *obs)


def shard_products(index_ref, grouped_ref, error_ref, misfit_ref, products_ref):
    members = misfit_ref.shape[0]
    half_rows = SUBLANES // 2

    def lines(first):
        return jnp.concatenate(
            [grouped_ref[pl.ds(first + q, members, stride=PACK_ROWS), :] for q in range(half_rows)],
            axis=1,
        )

    grouped, misfit = lines(0), lines(half_rows)
    misfit_ref[...] = misfit
    error = jnp.concatenate(
        [error_ref[pl.ds(index_ref[0] * half_rows + q, 1), :] for q in range(half_rows)], axis=1
    )
    anomaly = grouped - jnp.sum(grouped, axis=0, keepdims=True) * (1.0 / members)
    weighted = anomaly / error
    blank = jnp.zeros((LANES - 2 * members, grouped.shape[1]), jnp.float32)
    products_ref[...] = lax.dot_general(
        weighted,
        jnp.concatenate([misfit, anomaly, blank], axis=0),
        (((1,), (1,)), ((), ())),
        precision=lax.Precision.HIGHEST,
        preferred_element_type=jnp.float32,
    )


def solve_and_combine(total_obs, *refs):
    *product_refs, grouped_ref, out_ref = refs
    members = product_refs[0].shape[0]
    piece = PACK_ROWS - SUBLANES
    row = lax.broadcasted_iota(jnp.int32, (members, LANES), 0)
    lane = lax.broadcasted_iota(jnp.int32, (members, LANES), 1)
    system = product_refs[0][...]
    for ref in product_refs[1:]:
        system = system + ref[...]
    system = system / total_obs + jnp.where(row + members == lane, 1.0, 0.0)
    for k in range(members):
        at = slice(members + k, members + k + 1)
        pivot_row = system[k : k + 1, :] * (1.0 / system[k : k + 1, at])
        system = jnp.where(row == k, pivot_row, system - system[:, at] * pivot_row)
    coefficients = system[:, :members]
    combination = coefficients - jnp.sum(coefficients, axis=0, keepdims=True) * (1.0 / members)
    combination = combination + jnp.where(row == lane, 1.0, 0.0)[:, :members]
    weights = jnp.concatenate(
        [grouped_ref[pl.ds(SUBLANES + s, members, stride=PACK_ROWS), :] for s in range(piece)],
        axis=1,
    )
    combined = lax.dot_general(
        combination,
        weights,
        (((0,), (0,)), ((), ())),
        precision=lax.Precision.HIGHEST,
        preferred_element_type=jnp.float32,
    )
    for s in range(piece):
        out_ref[pl.ds(s, members, stride=piece), :] = combined[:, s * LANES : (s + 1) * LANES]


def combine(total_obs, products, grouped):
    members = products[0].shape[0]
    vmem = pl.BlockSpec(memory_space=pltpu.VMEM)
    return pl.pallas_call(
        functools.partial(solve_and_combine, total_obs),
        in_specs=[vmem] * (len(products) + 1),
        out_specs=vmem,
        out_shape=jax.ShapeDtypeStruct((members * (PACK_ROWS - SUBLANES), LANES), jnp.float32),
        compiler_params=pltpu.CompilerParams(vmem_limit_bytes=SMALL_VMEM_BYTES),
        name="solve_and_combine",
    )(*products, grouped)


def exchange(array, axis, moves):
    return [array] + [lax.ppermute(array, axis, list(enumerate(move))) for move in moves]


def on_device(
    state,
    weights,
    land_mask,
    level_gain,
    depth,
    obs_row,
    obs_col,
    obs_quad,
    obs_frac,
    obs_value,
    obs_error,
    noise,
):
    axes = ("half", "member")
    members = lax.axis_size(axes)
    index = lax.axis_index(axes).astype(jnp.int32).reshape(1)
    chips = lax.axis_size("member")
    side = math.isqrt(chips)
    tile_count = lax.axis_size("tile")
    obs_local = obs_row.shape[0]
    total_obs = obs_local * tile_count
    own = state[0]
    up = [(i, i + 1) for i in range(tile_count - 1)]
    down = [(target, source) for source, target in up]
    low = lax.ppermute(own[:, -1:], "tile", up)
    high = lax.ppermute(own[:, :1], "tile", down)
    grid = (obs_local // LANES, LANES)
    obs = (
        obs_row.reshape(grid),
        obs_col.reshape(grid),
        obs_quad.reshape(grid),
        obs_frac,
        obs_value.reshape(grid),
        noise.reshape(grid),
    )
    stepped, sampled = forward(level_gain, depth, own, low, high, weights[0], land_mask, obs)
    grouped = lax.all_to_all(
        sampled.reshape(members, PACK_ROWS, LANES), axes, split_axis=0, concat_axis=0, tiled=True
    )
    grouped = grouped.reshape(members * PACK_ROWS, LANES)
    vmem = pl.BlockSpec(memory_space=pltpu.VMEM)
    misfit, products = pl.pallas_call(
        shard_products,
        in_specs=[pl.BlockSpec(memory_space=pltpu.SMEM), vmem, vmem],
        out_specs=[vmem, vmem],
        out_shape=[
            jax.ShapeDtypeStruct((members, obs_local // members), jnp.float32),
            jax.ShapeDtypeStruct((members, LANES), jnp.float32),
        ],
        compiler_params=pltpu.CompilerParams(vmem_limit_bytes=SMALL_VMEM_BYTES),
        name="shard_products",
    )(index, grouped, obs_error.reshape(grid))

    def along_x(shift):
        return [(m // side) * side + (m % side + shift) % side for m in range(chips)]

    def along_y(shift):
        return [(m + shift * side) % chips for m in range(chips)]

    def along_z(shift):
        return [(t + shift) % tile_count for t in range(tile_count)]

    products = sum(exchange(products, "half", [(1, 0)]))
    products = sum(exchange(products, "member", [along_x(s) for s in (1, 3, 2)]))
    products = sum(exchange(products, "member", [along_y(s) for s in (1, 3, 2)]))
    products = sum(exchange(products, "tile", [along_z(1)]))
    products = exchange(products, "tile", [along_z(s) for s in (2, 6, 4)])
    combined = combine(total_obs, products, grouped)
    tiles = lax.all_to_all(
        combined.reshape(members, PACK_ROWS - SUBLANES, LANES),
        axes,
        split_axis=0,
        concat_axis=0,
        tiled=True,
    )
    _, rows, cols = weights.shape
    new_weights = (
        tiles.reshape(rows // SUBLANES, cols // LANES, SUBLANES, LANES)
        .transpose(0, 2, 1, 3)
        .reshape(weights.shape)
    )
    return (stepped[None], new_weights, misfit)


def solution(mesh):
    in_specs = (
        P(("half", "member"), None, "tile", None),
        P(("half", "member"), "tile", None),
        P("tile", None),
        P(),
        P(),
        P("tile"),
        P("tile"),
        P("tile"),
        P(None, "tile"),
        P("tile"),
        P("tile"),
        P(("half", "member"), "tile"),
    )
    out_specs = (
        P(("half", "member"), None, "tile", None),
        P(("half", "member"), "tile", None),
        P(None, ("half", "member", "tile")),
    )
    return jax.shard_map(
        on_device, mesh=mesh, in_specs=in_specs, out_specs=out_specs, check_vma=False
    )
```

```python
import functools
import math

import jax
import jax.numpy as jnp
from jax import lax
from jax.experimental import pallas as pl
from jax.experimental.pallas import tpu as pltpu
from jax.sharding import PartitionSpec as P

LANES = 128
SUBLANES = 8
LEVELS_STEP = 8
OBS_STEP = 2048
KEYS = 256
PACK_ROWS = 3 * SUBLANES
VMEM_BYTES = 60 * 1024 * 1024
SMALL_VMEM_BYTES = 8 * 1024 * 1024


def pick(table, index):
    return jnp.take_along_axis(table, index, axis=1, mode="promise_in_bounds")


def step_and_sample(
    gain_ref,
    depth_ref,
    state_ref,
    low_ref,
    high_ref,
    weights_ref,
    land_ref,
    row_ref,
    col_ref,
    quad_ref,
    frac_ref,
    value_ref,
    noise_ref,
    stepped_ref,
    sampled_ref,
    diffusivity_ref,
    column_ref,
    even_ref,
    odd_ref,
):
    step = pl.program_id(0)
    steps = pl.num_programs(0)
    levels, rows, cols = state_ref.shape
    sub = lax.broadcasted_iota(jnp.int32, (SUBLANES, cols), 0)

    @pl.when(step == 0)
    def _():
        diffusivity_ref[...] = land_ref[...].astype(jnp.float32) * (
            0.24 * jax.nn.sigmoid(weights_ref[...])
        )
        column_ref[...] = jnp.zeros_like(column_ref)
        for tile in range(rows * cols // (SUBLANES * LANES)):
            at_row, at_col = divmod(tile * LANES, cols)
            to = (tile // 2) * PACK_ROWS + (1 + tile % 2) * SUBLANES
            sampled_ref[pl.ds(to, SUBLANES), :] = weights_ref[
                pl.ds(at_row * SUBLANES, SUBLANES), pl.ds(at_col, LANES)
            ]

    for start in range(0, rows, SUBLANES):
        here = pl.ds(start, SUBLANES)
        total = column_ref[here, :]
        diffusivity = diffusivity_ref[here, :]
        for level in range(levels):
            centre = state_ref[level, here, :]
            if start == 0:
                above_row = low_ref[level]
            else:
                above_row = state_ref[level, pl.ds(start - 1, 1), :]
            if start + SUBLANES == rows:
                below_row = high_ref[level]
            else:
                below_row = state_ref[level, pl.ds(start + SUBLANES, 1), :]
            above = jnp.where(sub == 0, above_row, pltpu.roll(centre, 1, 0))
            below = jnp.where(
                sub == SUBLANES - 1, below_row, pltpu.roll(centre, SUBLANES - 1, 0)
            )
            laplacian = (
                above
                + below
                + pltpu.roll(centre, 1, 1)
                + pltpu.roll(centre, cols - 1, 1)
                - 4.0 * centre
            )
            number = step * levels + level
            stepped = centre + gain_ref[number] * diffusivity * laplacian
            stepped_ref[level, here, :] = stepped
            total = total + depth_ref[number] * stepped
        column_ref[here, :] = total

    @pl.when(step == steps - 1)
    def _():
        scale = 1.0 / math.sqrt(levels * steps)
        lane = lax.broadcasted_iota(jnp.int32, (SUBLANES, LANES), 1)
        doubled = (2 * lane) % LANES
        first_half = lane < LANES // 2
        for block in range(cols // (2 * LANES)):
            evens, odds = [], []
            for start in range(0, rows, SUBLANES):
                here = pl.ds(start, SUBLANES)
                left = column_ref[here, pl.ds(2 * block * LANES, LANES)] * scale
                right = column_ref[here, pl.ds((2 * block + 1) * LANES, LANES)] * scale
                evens.append(jnp.where(first_half, pick(left, doubled), pick(right, doubled)))
                odds.append(
                    jnp.where(first_half, pick(left, doubled + 1), pick(right, doubled + 1))
                )
            part, key = divmod(block * LANES, KEYS)
            for ref, pieces in ((even_ref, evens), (odd_ref, odds)):
                table = jnp.concatenate(pieces, axis=0)
                coarse = table.astype(jnp.bfloat16)
                fine = (table - coarse.astype(jnp.float32)).astype(jnp.bfloat16)
                ref[pl.ds(2 * part * rows, rows), pl.ds(key, LANES)] = coarse
                ref[pl.ds((2 * part + 1) * rows, rows), pl.ds(key, LANES)] = fine

        count = OBS_STEP // LANES
        keys = lax.broadcasted_iota(jnp.int32, (KEYS, OBS_STEP), 0)
        grid_row = lax.broadcasted_iota(jnp.int32, (rows, OBS_STEP), 0)
        shard_rows = SUBLANES // 2

        def look_up(ref, at):
            chosen = jnp.where(keys == (at & (KEYS - 1)), 1.0, 0.0).astype(jnp.bfloat16)
            found = jnp.dot(ref[...], chosen, preferred_element_type=jnp.float32)
            result = found[:rows] + found[rows : 2 * rows]
            for part in range(1, cols // (2 * KEYS)):
                base = 2 * part * rows
                other = found[base : base + rows] + found[base + rows : base + 2 * rows]
                result = jnp.where(at // KEYS == part, other, result)
            return result

        def sample(i, carry):
            def line(ref):
                return jnp.concatenate(
                    [ref[pl.ds(i * count + q, 1), :] for q in range(count)], axis=1
                )

            row, col, quad = line(row_ref), line(col_ref), line(quad_ref)
            place = pl.ds(pl.multiple_of(i * OBS_STEP, OBS_STEP), OBS_STEP)
            first = frac_ref[pl.ds(0, 1), place]
            second = frac_ref[pl.ds(1, 1), place]
            row_other = row + jnp.where((quad & 1) == 1, 1, -1)
            col_other = (col + jnp.where((quad >> 1) == 1, 1, -1)) & (cols - 1)
            is_even = (col & 1) == 0
            even_at = jnp.where(is_even, col, col_other) >> 1
            odd_at = jnp.where(is_even, col_other, col) >> 1
            even_by = jnp.where(is_even, 1.0 - second, second)
            odd_by = jnp.where(is_even, second, 1.0 - second)
            along = even_by * look_up(even_ref, even_at) + odd_by * look_up(odd_ref, odd_at)
            by_row = jnp.where(
                grid_row == row, 1.0 - first, jnp.where(grid_row == row_other, first, 0.0)
            )
            predicted = jnp.sum(by_row * along, axis=0, keepdims=True)
            residual = line(value_ref) + line(noise_ref) - predicted
            for q in range(count):
                shard, inner = divmod(q, shard_rows)
                to = (i * (count // shard_rows) + shard) * PACK_ROWS + inner
                lanes = slice(q * LANES, (q + 1) * LANES)
                sampled_ref[pl.ds(to, 1), :] = predicted[:, lanes]
                sampled_ref[pl.ds(to + shard_rows, 1), :] = residual[:, lanes]
            return carry

        lax.fori_loop(0, row_ref.shape[0] // count, sample, 0)


def forward(level_gain, depth, state, low, high, weights, land_mask, obs):
    levels, rows, cols = state.shape
    per = LEVELS_STEP
    packed = (obs[0].shape[0] // (SUBLANES // 2) * PACK_ROWS, LANES)

    def whole(shape):
        return pl.BlockSpec(shape, lambda i: (0,) * len(shape))

    smem = pl.BlockSpec(memory_space=pltpu.SMEM)
    halo = pl.BlockSpec((per, 1, cols), lambda i: (i, 0, 0))
    field = pl.BlockSpec((per, rows, cols), lambda i: (i, 0, 0))
    table = pltpu.VMEM((2 * rows * cols // (2 * KEYS), KEYS), jnp.bfloat16)
    return pl.pallas_call(
        step_and_sample,
        grid=(levels // per,),
        in_specs=[smem, smem, field, halo, halo]
        + [whole(array.shape) for array in (weights, land_mask, *obs)],
        out_specs=[field, whole(packed)],
        out_shape=[
            jax.ShapeDtypeStruct(state.shape, jnp.float32),
            jax.ShapeDtypeStruct(packed, jnp.float32),
        ],
        scratch_shapes=[
            pltpu.VMEM((rows, cols), jnp.float32),
            pltpu.VMEM((rows, cols), jnp.float32),
            table,
            table,
        ],
        compiler_params=pltpu.CompilerParams(vmem_limit_bytes=VMEM_BYTES),
        name="step_and_sample",
    )(level_gain, depth, state, low, high, weights, land_mask, *obs)


def shard_products(index_ref, grouped_ref, error_ref, misfit_ref, products_ref):
    members = misfit_ref.shape[0]
    half_rows = SUBLANES // 2

    def lines(first):
        return jnp.concatenate(
            [grouped_ref[pl.ds(first + q, members, stride=PACK_ROWS), :] for q in range(half_rows)],
            axis=1,
        )

    grouped, misfit = lines(0), lines(half_rows)
    misfit_ref[...] = misfit
    error = jnp.concatenate(
        [error_ref[pl.ds(index_ref[0] * half_rows + q, 1), :] for q in range(half_rows)], axis=1
    )
    anomaly = grouped - jnp.sum(grouped, axis=0, keepdims=True) * (1.0 / members)
    weighted = anomaly / error
    blank = jnp.zeros((LANES - 2 * members, grouped.shape[1]), jnp.float32)
    products = lax.dot_general(
        weighted,
        jnp.concatenate([misfit, anomaly, blank], axis=0),
        (((1,), (1,)), ((), ())),
        precision=lax.Precision.HIGHEST,
        preferred_element_type=jnp.float32,
    )
    half = members // 2
    packed = jnp.concatenate(
        [products[:half, : 2 * members], products[half:, : 2 * members]], axis=1
    )
    for receiver in range(products_ref.shape[0] // half):
        products_ref[pl.ds(receiver * half, half), :] = packed


def total_of(ref, rows):
    total = ref[pl.ds(0, rows), :]
    for sender in range(1, ref.shape[0] // rows):
        total = total + ref[pl.ds(sender * rows, rows), :]
    return total


def sum_and_spread(rows, parts_ref, out_ref):
    total = total_of(parts_ref, rows)
    for receiver in range(out_ref.shape[0] // rows):
        out_ref[pl.ds(receiver * rows, rows), :] = total


def solve_and_combine(total_obs, parts_ref, grouped_ref, out_ref):
    piece = PACK_ROWS - SUBLANES
    members = out_ref.shape[0] // piece
    packed = total_of(parts_ref, members // 2)
    row = lax.broadcasted_iota(jnp.int32, (members, 2 * members), 0)
    lane = lax.broadcasted_iota(jnp.int32, (members, 2 * members), 1)
    system = jnp.concatenate([packed[:, : 2 * members], packed[:, 2 * members :]], axis=0)
    system = system / total_obs + jnp.where(row + members == lane, 1.0, 0.0)
    for k in range(members):
        at = slice(members + k, members + k + 1)
        pivot_row = system[k : k + 1, :] * (1.0 / system[k : k + 1, at])
        system = jnp.where(row == k, pivot_row, system - system[:, at] * pivot_row)
    coefficients = system[:, :members]
    combination = coefficients - jnp.sum(coefficients, axis=0, keepdims=True) * (1.0 / members)
    combination = combination + jnp.where(row == lane, 1.0, 0.0)[:, :members]
    weights = jnp.concatenate(
        [grouped_ref[pl.ds(SUBLANES + s, members, stride=PACK_ROWS), :] for s in range(piece)],
        axis=1,
    )
    combined = lax.dot_general(
        combination,
        weights,
        (((0,), (0,)), ((), ())),
        precision=lax.Precision.HIGHEST,
        preferred_element_type=jnp.float32,
    )
    for s in range(piece):
        out_ref[pl.ds(s, members, stride=piece), :] = combined[:, s * LANES : (s + 1) * LANES]


def local(kernel, name, out_shapes, *args):
    vmem = pl.BlockSpec(memory_space=pltpu.VMEM)
    smem = pl.BlockSpec(memory_space=pltpu.SMEM)
    return pl.pallas_call(
        kernel,
        in_specs=[smem if array.dtype == jnp.int32 else vmem for array in args],
        out_specs=[vmem] * len(out_shapes),
        out_shape=[jax.ShapeDtypeStruct(shape, jnp.float32) for shape in out_shapes],
        compiler_params=pltpu.CompilerParams(vmem_limit_bytes=SMALL_VMEM_BYTES),
        name=name,
    )(*args)


def swap(array, axes):
    count = lax.axis_size(axes)
    pieces = array.reshape(count, array.shape[0] // count, array.shape[1])
    moved = lax.all_to_all(pieces, axes, split_axis=0, concat_axis=0, tiled=True)
    return moved.reshape(array.shape)


def on_device(
    state,
    weights,
    land_mask,
    level_gain,
    depth,
    obs_row,
    obs_col,
    obs_quad,
    obs_frac,
    obs_value,
    obs_error,
    noise,
):
    axes = ("half", "member")
    members = lax.axis_size(axes)
    index = lax.axis_index(axes).astype(jnp.int32).reshape(1)
    tile_count = lax.axis_size("tile")
    obs_local = obs_row.shape[0]
    total_obs = obs_local * tile_count
    own = state[0]
    up = [(i, i + 1) for i in range(tile_count - 1)]
    down = [(target, source) for source, target in up]
    low = lax.ppermute(own[:, -1:], "tile", up)
    high = lax.ppermute(own[:, :1], "tile", down)
    grid = (obs_local // LANES, LANES)
    obs = (
        obs_row.reshape(grid),
        obs_col.reshape(grid),
        obs_quad.reshape(grid),
        obs_frac,
        obs_value.reshape(grid),
        noise.reshape(grid),
    )
    stepped, sampled = forward(level_gain, depth, own, low, high, weights[0], land_mask, obs)
    grouped = swap(sampled, axes)
    packed_rows = members // 2
    misfit, products = local(
        shard_products,
        "shard_products",
        [(members, obs_local // members), (members * packed_rows, LANES)],
        index,
        grouped,
        obs_error.reshape(grid),
    )
    (products,) = local(
        functools.partial(sum_and_spread, packed_rows),
        "sum_and_spread",
        [(tile_count * packed_rows, LANES)],
        swap(products, axes),
    )
    (combined,) = local(
        functools.partial(solve_and_combine, total_obs),
        "solve_and_combine",
        [(members * (PACK_ROWS - SUBLANES), LANES)],
        swap(products, "tile"),
        grouped,
    )
    tiles = swap(combined, axes)
    _, rows, cols = weights.shape
    new_weights = (
        tiles.reshape(rows // SUBLANES, cols // LANES, SUBLANES, LANES)
        .transpose(0, 2, 1, 3)
        .reshape(weights.shape)
    )
    return (stepped[None], new_weights, misfit)


def solution(mesh):
    in_specs = (
        P(("half", "member"), None, "tile", None),
        P(("half", "member"), "tile", None),
        P("tile", None),
        P(),
        P(),
        P("tile"),
        P("tile"),
        P("tile"),
        P(None, "tile"),
        P("tile"),
        P("tile"),
        P(("half", "member"), "tile"),
    )
    out_specs = (
        P(("half", "member"), None, "tile", None),
        P(("half", "member"), "tile", None),
        P(None, ("half", "member", "tile")),
    )
    return jax.shard_map(
        on_device, mesh=mesh, in_specs=in_specs, out_specs=out_specs, check_vma=False
    )
```

```python
import functools
import math

import jax
import jax.numpy as jnp
from jax import lax
from jax.experimental import pallas as pl
from jax.experimental.pallas import tpu as pltpu
from jax.sharding import PartitionSpec as P

LANES = 128
SUBLANES = 8
LEVELS_STEP = 4
OBS_STEP = 2048
KEYS = 256
PACK_ROWS = 3 * SUBLANES
VMEM_BYTES = 60 * 1024 * 1024
MIDDLE_VMEM_BYTES = 24 * 1024 * 1024
SMALL_VMEM_BYTES = 8 * 1024 * 1024


def pick(table, index):
    return jnp.take_along_axis(table, index, axis=1, mode="promise_in_bounds")


def diffusivity_of(land, weights):
    return land.astype(jnp.float32) * (0.24 * jax.nn.sigmoid(weights))


def laplacian_of(centre, above_row, below_row):
    cols = centre.shape[1]
    sub = lax.broadcasted_iota(jnp.int32, centre.shape, 0)
    above = jnp.where(sub == 0, above_row, pltpu.roll(centre, 1, 0))
    below = jnp.where(sub == SUBLANES - 1, below_row, pltpu.roll(centre, SUBLANES - 1, 0))
    return (
        above
        + below
        + pltpu.roll(centre, 1, 1)
        + pltpu.roll(centre, cols - 1, 1)
        - 4.0 * centre
    )


def sum_column(
    gain_ref, depth_ref, state_ref, weights_ref, land_ref, column_ref, held_ref, flow_ref, sems
):
    levels, rows, cols = state_ref.shape
    parts = sems.shape[0]
    per = levels // parts

    def copy(part):
        here = pl.ds(part * per, per)
        return pltpu.make_async_copy(state_ref.at[here], held_ref.at[here], sems.at[part])

    for part in range(parts):
        copy(part).start()
    for part in range(parts):
        copy(part).wait()
        for start in range(0, rows, SUBLANES):
            here = pl.ds(start, SUBLANES)
            column = flow = None
            for level in range(part * per, (part + 1) * per):
                weighted = depth_ref[level] * held_ref[level, here, :]
                moved = gain_ref[level] * weighted
                column = weighted if column is None else column + weighted
                flow = moved if flow is None else flow + moved
            if part > 0:
                column = column + column_ref[here, :]
                flow = flow + flow_ref[here, :]
            column_ref[here, :] = column
            flow_ref[here, :] = flow
    scale = 1.0 / math.sqrt(levels)
    blank = jnp.zeros((1, cols), jnp.float32)
    for start in range(0, rows, SUBLANES):
        here = pl.ds(start, SUBLANES)
        end = start + SUBLANES
        laplacian = laplacian_of(
            flow_ref[here, :],
            flow_ref[pl.ds(start - 1, 1), :] if start > 0 else blank,
            flow_ref[pl.ds(end, 1), :] if end < rows else blank,
        )
        diffusivity = diffusivity_of(land_ref[here, :], weights_ref[here, :])
        column_ref[here, :] = scale * (column_ref[here, :] + diffusivity * laplacian)


def has_neighbours(tile_count, tile_ref):
    tile = tile_ref[0]
    return jnp.where(tile > 0, 1.0, 0.0), jnp.where(tile < tile_count - 1, 1.0, 0.0)


def step_levels(
    tile_count, tile_ref, gain_ref, state_ref, low_ref, high_ref, weights_ref, land_ref, after_ref, stepped_ref,
    mark_ref, diffusivity_ref,
):
    del after_ref
    step = pl.program_id(0)
    levels, rows, cols = state_ref.shape
    has_low, has_high = has_neighbours(tile_count, tile_ref)

    @pl.when(step == 0)
    def _():
        diffusivity_ref[...] = diffusivity_of(land_ref[...], weights_ref[...])
        mark_ref[...] = jnp.zeros_like(mark_ref)

    for start in range(0, rows, SUBLANES):
        here = pl.ds(start, SUBLANES)
        end = start + SUBLANES
        for level in range(levels):
            centre = state_ref[level, here, :]
            laplacian = laplacian_of(
                centre,
                state_ref[level, pl.ds(start - 1, 1), :] if start > 0 else has_low * low_ref[level],
                state_ref[level, pl.ds(end, 1), :] if end < rows else has_high * high_ref[level],
            )
            factor = gain_ref[step * levels + level] * diffusivity_ref[here, :]
            stepped_ref[level, here, :] = centre + factor * laplacian


def sample_column(
    tile_count,
    tile_ref,
    gain_ref,
    depth_ref,
    column_ref,
    low_ref,
    high_ref,
    weights_ref,
    land_ref,
    row_ref,
    col_ref,
    quad_ref,
    frac_ref,
    value_ref,
    noise_ref,
    sampled_ref,
    even_ref,
    odd_ref,
):
    rows, cols = column_ref.shape
    levels = low_ref.shape[0]
    for tile in range(rows * cols // (SUBLANES * LANES)):
        at_row, at_col = divmod(tile * LANES, cols)
        to = (tile // 2) * PACK_ROWS + (1 + tile % 2) * SUBLANES
        sampled_ref[pl.ds(to, SUBLANES), :] = weights_ref[
            pl.ds(at_row * SUBLANES, SUBLANES), pl.ds(at_col, LANES)
        ]

    def edge(ref, row, factor):
        one = pl.ds(row, 1)
        flow = jnp.zeros((1, cols), jnp.float32)
        for level in range(levels):
            flow = flow + (gain_ref[level] * depth_ref[level]) * ref[level]
        diffusivity = diffusivity_of(land_ref[one, :], weights_ref[one, :])
        return (factor / math.sqrt(levels)) * diffusivity * flow

    has_low, has_high = has_neighbours(tile_count, tile_ref)
    low, high = edge(low_ref, 0, has_low), edge(high_ref, rows - 1, has_high)
    sub = lax.broadcasted_iota(jnp.int32, (SUBLANES, LANES), 0)

    def column_tile(start, first):
        tile = column_ref[pl.ds(start, SUBLANES), pl.ds(first, LANES)]
        lanes = slice(first, first + LANES)
        if start == 0:
            tile = tile + jnp.where(sub == 0, low[:, lanes], 0.0)
        if start + SUBLANES == rows:
            tile = tile + jnp.where(sub == SUBLANES - 1, high[:, lanes], 0.0)
        return tile

    lane = lax.broadcasted_iota(jnp.int32, (SUBLANES, LANES), 1)
    doubled = (2 * lane) % LANES
    first_half = lane < LANES // 2
    for block in range(cols // (2 * LANES)):
        evens, odds = [], []
        for start in range(0, rows, SUBLANES):
            left = column_tile(start, 2 * block * LANES)
            right = column_tile(start, (2 * block + 1) * LANES)
            evens.append(jnp.where(first_half, pick(left, doubled), pick(right, doubled)))
            odds.append(
                jnp.where(first_half, pick(left, doubled + 1), pick(right, doubled + 1))
            )
        part, key = divmod(block * LANES, KEYS)
        for ref, pieces in ((even_ref, evens), (odd_ref, odds)):
            table = jnp.concatenate(pieces, axis=0)
            coarse = table.astype(jnp.bfloat16)
            fine = (table - coarse.astype(jnp.float32)).astype(jnp.bfloat16)
            ref[pl.ds(2 * part * rows, rows), pl.ds(key, LANES)] = coarse
            ref[pl.ds((2 * part + 1) * rows, rows), pl.ds(key, LANES)] = fine

    count = OBS_STEP // LANES
    keys = lax.broadcasted_iota(jnp.int32, (KEYS, OBS_STEP), 0)
    grid_row = lax.broadcasted_iota(jnp.int32, (rows, OBS_STEP), 0)
    shard_rows = SUBLANES // 2

    def look_up(ref, at):
        chosen = jnp.where(keys == (at & (KEYS - 1)), 1.0, 0.0).astype(jnp.bfloat16)
        found = jnp.dot(ref[...], chosen, preferred_element_type=jnp.float32)
        result = found[:rows] + found[rows : 2 * rows]
        for part in range(1, cols // (2 * KEYS)):
            base = 2 * part * rows
            other = found[base : base + rows] + found[base + rows : base + 2 * rows]
            result = jnp.where(at // KEYS == part, other, result)
        return result

    def sample(i, carry):
        def line(ref):
            return jnp.concatenate(
                [ref[pl.ds(i * count + q, 1), :] for q in range(count)], axis=1
            )

        row, col, quad = line(row_ref), line(col_ref), line(quad_ref)
        place = pl.ds(pl.multiple_of(i * OBS_STEP, OBS_STEP), OBS_STEP)
        first = frac_ref[pl.ds(0, 1), place]
        second = frac_ref[pl.ds(1, 1), place]
        row_other = row + jnp.where((quad & 1) == 1, 1, -1)
        col_other = (col + jnp.where((quad >> 1) == 1, 1, -1)) & (cols - 1)
        is_even = (col & 1) == 0
        even_at = jnp.where(is_even, col, col_other) >> 1
        odd_at = jnp.where(is_even, col_other, col) >> 1
        even_by = jnp.where(is_even, 1.0 - second, second)
        odd_by = jnp.where(is_even, second, 1.0 - second)
        along = even_by * look_up(even_ref, even_at) + odd_by * look_up(odd_ref, odd_at)
        by_row = jnp.where(
            grid_row == row, 1.0 - first, jnp.where(grid_row == row_other, first, 0.0)
        )
        predicted = jnp.sum(by_row * along, axis=0, keepdims=True)
        residual = line(value_ref) + line(noise_ref) - predicted
        for q in range(count):
            shard, inner = divmod(q, shard_rows)
            to = (i * (count // shard_rows) + shard) * PACK_ROWS + inner
            lanes = slice(q * LANES, (q + 1) * LANES)
            sampled_ref[pl.ds(to, 1), :] = predicted[:, lanes]
            sampled_ref[pl.ds(to + shard_rows, 1), :] = residual[:, lanes]
        return carry

    lax.fori_loop(0, row_ref.shape[0] // count, sample, 0)


def forward(tile_count, tile, level_gain, depth, state, low, high, weights, land_mask, obs):
    levels, rows, cols = state.shape
    per = LEVELS_STEP
    packed = (obs[0].shape[0] // (SUBLANES // 2) * PACK_ROWS, LANES)
    smem = pl.BlockSpec(memory_space=pltpu.SMEM)
    vmem = pl.BlockSpec(memory_space=pltpu.VMEM)
    plane = pl.BlockSpec((rows, cols), lambda i: (0, 0))
    halo = pl.BlockSpec((per, 1, cols), lambda i: (i, 0, 0))
    field = pl.BlockSpec((per, rows, cols), lambda i: (i, 0, 0))
    column = pl.pallas_call(
        sum_column,
        in_specs=[smem, smem, pl.BlockSpec(memory_space=pl.ANY), vmem, vmem],
        out_specs=vmem,
        out_shape=jax.ShapeDtypeStruct((rows, cols), jnp.float32),
        scratch_shapes=[
            pltpu.VMEM(state.shape, jnp.float32),
            pltpu.VMEM((rows, cols), jnp.float32),
            pltpu.SemaphoreType.DMA((levels // per,)),
        ],
        compiler_params=pltpu.CompilerParams(vmem_limit_bytes=VMEM_BYTES),
        cost_estimate=pl.CostEstimate(
            flops=6 * state.size, bytes_accessed=4 * state.size, transcendentals=0
        ),
        name="sum_column",
    )(level_gain, depth, state, weights, land_mask)
    table = pltpu.VMEM((2 * rows * cols // (2 * KEYS), KEYS), jnp.bfloat16)
    sampled = pl.pallas_call(
        functools.partial(sample_column, tile_count),
        in_specs=[smem, smem, smem] + [vmem] * (5 + len(obs)),
        out_specs=vmem,
        out_shape=jax.ShapeDtypeStruct(packed, jnp.float32),
        scratch_shapes=[table, table],
        compiler_params=pltpu.CompilerParams(vmem_limit_bytes=MIDDLE_VMEM_BYTES),
        name="sample_column",
    )(tile, level_gain, depth, column, low, high, weights, land_mask, *obs)
    stepped, mark = pl.pallas_call(
        functools.partial(step_levels, tile_count),
        grid=(levels // per,),
        in_specs=[smem, smem, field, halo, halo, plane, plane, pl.BlockSpec(memory_space=pl.ANY)],
        out_specs=[field, pl.BlockSpec((SUBLANES, LANES), lambda i: (0, 0))],
        out_shape=[
            jax.ShapeDtypeStruct(state.shape, jnp.float32),
            jax.ShapeDtypeStruct((SUBLANES, LANES), jnp.float32),
        ],
        scratch_shapes=[pltpu.VMEM((rows, cols), jnp.float32)],
        compiler_params=pltpu.CompilerParams(vmem_limit_bytes=MIDDLE_VMEM_BYTES),
        cost_estimate=pl.CostEstimate(
            flops=10 * state.size, bytes_accessed=8 * state.size, transcendentals=0
        ),
        name="step_levels",
    )(tile, level_gain, state, low, high, weights, land_mask, sampled)
    return stepped, mark, sampled


def shard_products(index_ref, grouped_ref, error_ref, after_ref, misfit_ref, products_ref):
    del after_ref
    members = misfit_ref.shape[0]
    half_rows = SUBLANES // 2

    def lines(first):
        return jnp.concatenate(
            [grouped_ref[pl.ds(first + q, members, stride=PACK_ROWS), :] for q in range(half_rows)],
            axis=1,
        )

    grouped, misfit = lines(0), lines(half_rows)
    misfit_ref[...] = misfit
    error = jnp.concatenate(
        [error_ref[pl.ds(index_ref[0] * half_rows + q, 1), :] for q in range(half_rows)], axis=1
    )
    anomaly = grouped - jnp.sum(grouped, axis=0, keepdims=True) * (1.0 / members)
    weighted = anomaly / error
    blank = jnp.zeros((LANES - 2 * members, grouped.shape[1]), jnp.float32)
    products = lax.dot_general(
        weighted,
        jnp.concatenate([misfit, anomaly, blank], axis=0),
        (((1,), (1,)), ((), ())),
        precision=lax.Precision.HIGHEST,
        preferred_element_type=jnp.float32,
    )
    half = members // 2
    packed = jnp.concatenate(
        [products[:half, : 2 * members], products[half:, : 2 * members]], axis=1
    )
    for receiver in range(products_ref.shape[0] // half):
        products_ref[pl.ds(receiver * half, half), :] = packed


def total_of(ref, rows):
    total = ref[pl.ds(0, rows), :]
    for sender in range(1, ref.shape[0] // rows):
        total = total + ref[pl.ds(sender * rows, rows), :]
    return total


def sum_and_spread(rows, parts_ref, out_ref):
    total = total_of(parts_ref, rows)
    for receiver in range(out_ref.shape[0] // rows):
        out_ref[pl.ds(receiver * rows, rows), :] = total


def solve_and_combine(total_obs, parts_ref, grouped_ref, out_ref):
    piece = PACK_ROWS - SUBLANES
    members = out_ref.shape[0] // piece
    packed = total_of(parts_ref, members // 2)
    row = lax.broadcasted_iota(jnp.int32, (members, 2 * members), 0)
    lane = lax.broadcasted_iota(jnp.int32, (members, 2 * members), 1)
    system = jnp.concatenate([packed[:, : 2 * members], packed[:, 2 * members :]], axis=0)
    system = system / total_obs + jnp.where(row + members == lane, 1.0, 0.0)
    for k in range(members):
        at = slice(members + k, members + k + 1)
        pivot_row = system[k : k + 1, :] * (1.0 / system[k : k + 1, at])
        system = jnp.where(row == k, pivot_row, system - system[:, at] * pivot_row)
    coefficients = system[:, :members]
    combination = coefficients - jnp.sum(coefficients, axis=0, keepdims=True) * (1.0 / members)
    combination = combination + jnp.where(row == lane, 1.0, 0.0)[:, :members]
    weights = jnp.concatenate(
        [grouped_ref[pl.ds(SUBLANES + s, members, stride=PACK_ROWS), :] for s in range(piece)],
        axis=1,
    )
    combined = lax.dot_general(
        combination,
        weights,
        (((0,), (0,)), ((), ())),
        precision=lax.Precision.HIGHEST,
        preferred_element_type=jnp.float32,
    )
    for s in range(piece):
        out_ref[pl.ds(s, members, stride=piece), :] = combined[:, s * LANES : (s + 1) * LANES]


def local(kernel, name, out_shapes, *args):
    vmem = pl.BlockSpec(memory_space=pltpu.VMEM)
    smem = pl.BlockSpec(memory_space=pltpu.SMEM)
    return pl.pallas_call(
        kernel,
        in_specs=[smem if array.dtype == jnp.int32 else vmem for array in args],
        out_specs=[vmem] * len(out_shapes),
        out_shape=[jax.ShapeDtypeStruct(shape, jnp.float32) for shape in out_shapes],
        compiler_params=pltpu.CompilerParams(vmem_limit_bytes=SMALL_VMEM_BYTES),
        name=name,
    )(*args)


def swap(array, axes):
    count = lax.axis_size(axes)
    pieces = array.reshape(count, array.shape[0] // count, array.shape[1])
    moved = lax.all_to_all(pieces, axes, split_axis=0, concat_axis=0, tiled=True)
    return moved.reshape(array.shape)


def on_device(
    state,
    weights,
    land_mask,
    level_gain,
    depth,
    obs_row,
    obs_col,
    obs_quad,
    obs_frac,
    obs_value,
    obs_error,
    noise,
):
    axes = ("half", "member")
    members = lax.axis_size(axes)
    index = lax.axis_index(axes).astype(jnp.int32).reshape(1)
    tile_count = lax.axis_size("tile")
    obs_local = obs_row.shape[0]
    total_obs = obs_local * tile_count
    own = state[0]
    up = [(i, (i + 1) % tile_count) for i in range(tile_count)]
    down = [(target, source) for source, target in up]
    low = lax.ppermute(own[:, -1:], "tile", up)
    high = lax.ppermute(own[:, :1], "tile", down)
    tile = lax.axis_index("tile").astype(jnp.int32).reshape(1)
    grid = (obs_local // LANES, LANES)
    obs = (
        obs_row.reshape(grid),
        obs_col.reshape(grid),
        obs_quad.reshape(grid),
        obs_frac,
        obs_value.reshape(grid),
        noise.reshape(grid),
    )
    stepped, stepped_mark, sampled = forward(
        tile_count, tile, level_gain, depth, own, low, high, weights[0], land_mask, obs
    )
    grouped = swap(sampled, axes)
    packed_rows = members // 2
    misfit, products = local(
        shard_products,
        "shard_products",
        [(members, obs_local // members), (members * packed_rows, LANES)],
        index,
        grouped,
        obs_error.reshape(grid),
        stepped_mark,
    )
    (products,) = local(
        functools.partial(sum_and_spread, packed_rows),
        "sum_and_spread",
        [(tile_count * packed_rows, LANES)],
        swap(products, axes),
    )
    (combined,) = local(
        functools.partial(solve_and_combine, total_obs),
        "solve_and_combine",
        [(members * (PACK_ROWS - SUBLANES), LANES)],
        swap(products, "tile"),
        grouped,
    )
    tiles = swap(combined, axes)
    _, rows, cols = weights.shape
    new_weights = (
        tiles.reshape(rows // SUBLANES, cols // LANES, SUBLANES, LANES)
        .transpose(0, 2, 1, 3)
        .reshape(weights.shape)
    )
    return (stepped[None], new_weights, misfit)


def solution(mesh):
    in_specs = (
        P(("half", "member"), None, "tile", None),
        P(("half", "member"), "tile", None),
        P("tile", None),
        P(),
        P(),
        P("tile"),
        P("tile"),
        P("tile"),
        P(None, "tile"),
        P("tile"),
        P("tile"),
        P(("half", "member"), "tile"),
    )
    out_specs = (
        P(("half", "member"), None, "tile", None),
        P(("half", "member"), "tile", None),
        P(None, ("half", "member", "tile")),
    )
    return jax.shard_map(
        on_device, mesh=mesh, in_specs=in_specs, out_specs=out_specs, check_vma=False
    )
```

```python
import functools
import math

import jax
import jax.numpy as jnp
from jax import lax
from jax.experimental import pallas as pl
from jax.experimental.pallas import tpu as pltpu
from jax.sharding import PartitionSpec as P

LANES = 128
SUBLANES = 8
LEVELS_STEP = 4
OBS_STEP = 2048
KEYS = 256
PACK_ROWS = 3 * SUBLANES
VMEM_BYTES = 60 * 1024 * 1024
MIDDLE_VMEM_BYTES = 24 * 1024 * 1024
SMALL_VMEM_BYTES = 8 * 1024 * 1024


def pick(table, index):
    return jnp.take_along_axis(table, index, axis=1, mode="promise_in_bounds")


def diffusivity_of(land, weights):
    return land.astype(jnp.float32) * (0.24 * jax.nn.sigmoid(weights))


def laplacian_of(centre, above_row, below_row):
    cols = centre.shape[1]
    sub = lax.broadcasted_iota(jnp.int32, centre.shape, 0)
    above = jnp.where(sub == 0, above_row, pltpu.roll(centre, 1, 0))
    below = jnp.where(sub == SUBLANES - 1, below_row, pltpu.roll(centre, SUBLANES - 1, 0))
    return (
        above
        + below
        + pltpu.roll(centre, 1, 1)
        + pltpu.roll(centre, cols - 1, 1)
        - 4.0 * centre
    )


def sum_column(
    gain_ref,
    depth_ref,
    state_ref,
    weights_far_ref,
    land_far_ref,
    column_ref,
    held_ref,
    flow_ref,
    weights_ref,
    land_ref,
    sems,
):
    levels, rows, cols = state_ref.shape
    parts = sems.shape[0] - 2
    per = levels // parts

    def copy(part):
        here = pl.ds(part * per, per)
        return pltpu.make_async_copy(state_ref.at[here], held_ref.at[here], sems.at[part])

    planes = [
        pltpu.make_async_copy(weights_far_ref, weights_ref, sems.at[parts]),
        pltpu.make_async_copy(land_far_ref, land_ref, sems.at[parts + 1]),
    ]
    for part in range(parts):
        copy(part).start()
    for plane in planes:
        plane.start()
    for part in range(parts):
        copy(part).wait()
        for start in range(0, rows, SUBLANES):
            here = pl.ds(start, SUBLANES)
            column = flow = None
            for level in range(part * per, (part + 1) * per):
                weighted = depth_ref[level] * held_ref[level, here, :]
                moved = gain_ref[level] * weighted
                column = weighted if column is None else column + weighted
                flow = moved if flow is None else flow + moved
            if part > 0:
                column = column + column_ref[here, :]
                flow = flow + flow_ref[here, :]
            column_ref[here, :] = column
            flow_ref[here, :] = flow
    for plane in planes:
        plane.wait()
    scale = 1.0 / math.sqrt(levels)
    blank = jnp.zeros((1, cols), jnp.float32)
    for start in range(0, rows, SUBLANES):
        here = pl.ds(start, SUBLANES)
        end = start + SUBLANES
        laplacian = laplacian_of(
            flow_ref[here, :],
            flow_ref[pl.ds(start - 1, 1), :] if start > 0 else blank,
            flow_ref[pl.ds(end, 1), :] if end < rows else blank,
        )
        diffusivity = diffusivity_of(land_ref[here, :], weights_ref[here, :])
        column_ref[here, :] = scale * (column_ref[here, :] + diffusivity * laplacian)


def has_neighbours(tile_count, tile_ref):
    tile = tile_ref[0]
    return jnp.where(tile > 0, 1.0, 0.0), jnp.where(tile < tile_count - 1, 1.0, 0.0)


def step_levels(
    tile_count, tile_ref, gain_ref, state_ref, low_ref, high_ref, weights_ref, land_ref, after_ref, stepped_ref,
    mark_ref, diffusivity_ref,
):
    del after_ref
    step = pl.program_id(0)
    levels, rows, cols = state_ref.shape
    has_low, has_high = has_neighbours(tile_count, tile_ref)

    @pl.when(step == 0)
    def _():
        diffusivity_ref[...] = diffusivity_of(land_ref[...], weights_ref[...])
        mark_ref[...] = jnp.zeros_like(mark_ref)

    for start in range(0, rows, SUBLANES):
        here = pl.ds(start, SUBLANES)
        end = start + SUBLANES
        for level in range(levels):
            centre = state_ref[level, here, :]
            laplacian = laplacian_of(
                centre,
                state_ref[level, pl.ds(start - 1, 1), :] if start > 0 else has_low * low_ref[level],
                state_ref[level, pl.ds(end, 1), :] if end < rows else has_high * high_ref[level],
            )
            factor = gain_ref[step * levels + level] * diffusivity_ref[here, :]
            stepped_ref[level, here, :] = centre + factor * laplacian


def sample_column(
    tile_count,
    tile_ref,
    gain_ref,
    depth_ref,
    column_ref,
    low_ref,
    high_ref,
    weights_ref,
    land_ref,
    row_ref,
    col_ref,
    quad_ref,
    frac_ref,
    value_ref,
    noise_ref,
    sampled_ref,
    even_ref,
    odd_ref,
):
    rows, cols = column_ref.shape
    levels = low_ref.shape[0]
    for tile in range(rows * cols // (SUBLANES * LANES)):
        at_row, at_col = divmod(tile * LANES, cols)
        to = (tile // 2) * PACK_ROWS + (1 + tile % 2) * SUBLANES
        sampled_ref[pl.ds(to, SUBLANES), :] = weights_ref[
            pl.ds(at_row * SUBLANES, SUBLANES), pl.ds(at_col, LANES)
        ]

    def edge(ref, row, factor):
        one = pl.ds(row, 1)
        flow = jnp.zeros((1, cols), jnp.float32)
        for level in range(levels):
            flow = flow + (gain_ref[level] * depth_ref[level]) * ref[level]
        diffusivity = diffusivity_of(land_ref[one, :], weights_ref[one, :])
        return (factor / math.sqrt(levels)) * diffusivity * flow

    has_low, has_high = has_neighbours(tile_count, tile_ref)
    low, high = edge(low_ref, 0, has_low), edge(high_ref, rows - 1, has_high)
    sub = lax.broadcasted_iota(jnp.int32, (SUBLANES, LANES), 0)

    def column_tile(start, first):
        tile = column_ref[pl.ds(start, SUBLANES), pl.ds(first, LANES)]
        lanes = slice(first, first + LANES)
        if start == 0:
            tile = tile + jnp.where(sub == 0, low[:, lanes], 0.0)
        if start + SUBLANES == rows:
            tile = tile + jnp.where(sub == SUBLANES - 1, high[:, lanes], 0.0)
        return tile

    lane = lax.broadcasted_iota(jnp.int32, (SUBLANES, LANES), 1)
    doubled = (2 * lane) % LANES
    first_half = lane < LANES // 2
    for block in range(cols // (2 * LANES)):
        evens, odds = [], []
        for start in range(0, rows, SUBLANES):
            left = column_tile(start, 2 * block * LANES)
            right = column_tile(start, (2 * block + 1) * LANES)
            evens.append(jnp.where(first_half, pick(left, doubled), pick(right, doubled)))
            odds.append(
                jnp.where(first_half, pick(left, doubled + 1), pick(right, doubled + 1))
            )
        part, key = divmod(block * LANES, KEYS)
        for ref, pieces in ((even_ref, evens), (odd_ref, odds)):
            table = jnp.concatenate(pieces, axis=0)
            coarse = table.astype(jnp.bfloat16)
            fine = (table - coarse.astype(jnp.float32)).astype(jnp.bfloat16)
            ref[pl.ds(2 * part * rows, rows), pl.ds(key, LANES)] = coarse
            ref[pl.ds((2 * part + 1) * rows, rows), pl.ds(key, LANES)] = fine

    count = OBS_STEP // LANES
    keys = lax.broadcasted_iota(jnp.int16, (KEYS, OBS_STEP), 0)
    one, zero = jnp.bfloat16(1.0), jnp.bfloat16(0.0)
    grid_row = lax.broadcasted_iota(jnp.int32, (rows, OBS_STEP), 0)
    shard_rows = SUBLANES // 2

    def look_up(ref, at):
        chosen = jnp.where(keys == (at & (KEYS - 1)).astype(jnp.int16), one, zero)
        found = jnp.dot(ref[...], chosen, preferred_element_type=jnp.float32)
        result = found[:rows] + found[rows : 2 * rows]
        for part in range(1, cols // (2 * KEYS)):
            base = 2 * part * rows
            other = found[base : base + rows] + found[base + rows : base + 2 * rows]
            result = jnp.where(at // KEYS == part, other, result)
        return result

    def sample(i, carry):
        def line(ref):
            return jnp.concatenate(
                [ref[pl.ds(i * count + q, 1), :] for q in range(count)], axis=1
            )

        row, col, quad = line(row_ref), line(col_ref), line(quad_ref)
        place = pl.ds(pl.multiple_of(i * OBS_STEP, OBS_STEP), OBS_STEP)
        first = frac_ref[pl.ds(0, 1), place]
        second = frac_ref[pl.ds(1, 1), place]
        row_other = row + jnp.where((quad & 1) == 1, 1, -1)
        col_other = (col + jnp.where((quad >> 1) == 1, 1, -1)) & (cols - 1)
        is_even = (col & 1) == 0
        even_at = jnp.where(is_even, col, col_other) >> 1
        odd_at = jnp.where(is_even, col_other, col) >> 1
        even_by = jnp.where(is_even, 1.0 - second, second)
        odd_by = jnp.where(is_even, second, 1.0 - second)
        along = even_by * look_up(even_ref, even_at) + odd_by * look_up(odd_ref, odd_at)
        by_row = jnp.where(
            grid_row == row, 1.0 - first, jnp.where(grid_row == row_other, first, 0.0)
        )
        predicted = jnp.sum(by_row * along, axis=0, keepdims=True)
        residual = line(value_ref) + line(noise_ref) - predicted
        for q in range(count):
            shard, inner = divmod(q, shard_rows)
            to = (i * (count // shard_rows) + shard) * PACK_ROWS + inner
            lanes = slice(q * LANES, (q + 1) * LANES)
            sampled_ref[pl.ds(to, 1), :] = predicted[:, lanes]
            sampled_ref[pl.ds(to + shard_rows, 1), :] = residual[:, lanes]
        return carry

    lax.fori_loop(0, row_ref.shape[0] // count, sample, 0)


def forward(tile_count, tile, level_gain, depth, state, low, high, weights, land_mask, obs):
    levels, rows, cols = state.shape
    per = LEVELS_STEP
    packed = (obs[0].shape[0] // (SUBLANES // 2) * PACK_ROWS, LANES)
    smem = pl.BlockSpec(memory_space=pltpu.SMEM)
    vmem = pl.BlockSpec(memory_space=pltpu.VMEM)
    plane = pl.BlockSpec((rows, cols), lambda i: (0, 0))
    halo = pl.BlockSpec((per, 1, cols), lambda i: (i, 0, 0))
    field = pl.BlockSpec((per, rows, cols), lambda i: (i, 0, 0))
    column = pl.pallas_call(
        sum_column,
        in_specs=[smem, smem] + [pl.BlockSpec(memory_space=pl.ANY)] * 3,
        out_specs=vmem,
        out_shape=jax.ShapeDtypeStruct((rows, cols), jnp.float32),
        scratch_shapes=[
            pltpu.VMEM(state.shape, jnp.float32),
            pltpu.VMEM((rows, cols), jnp.float32),
            pltpu.VMEM((rows, cols), jnp.float32),
            pltpu.VMEM((rows, cols), jnp.int32),
            pltpu.SemaphoreType.DMA((levels // per + 2,)),
        ],
        compiler_params=pltpu.CompilerParams(vmem_limit_bytes=VMEM_BYTES),
        cost_estimate=pl.CostEstimate(
            flops=6 * state.size, bytes_accessed=4 * state.size, transcendentals=0
        ),
        name="sum_column",
    )(level_gain, depth, state, weights, land_mask)
    table = pltpu.VMEM((2 * rows * cols // (2 * KEYS), KEYS), jnp.bfloat16)
    sampled = pl.pallas_call(
        functools.partial(sample_column, tile_count),
        in_specs=[smem, smem, smem] + [vmem] * (5 + len(obs)),
        out_specs=vmem,
        out_shape=jax.ShapeDtypeStruct(packed, jnp.float32),
        scratch_shapes=[table, table],
        compiler_params=pltpu.CompilerParams(vmem_limit_bytes=MIDDLE_VMEM_BYTES),
        name="sample_column",
    )(tile, level_gain, depth, column, low, high, weights, land_mask, *obs)
    stepped, mark = pl.pallas_call(
        functools.partial(step_levels, tile_count),
        grid=(levels // per,),
        in_specs=[smem, smem, field, halo, halo, plane, plane, pl.BlockSpec(memory_space=pl.ANY)],
        out_specs=[field, pl.BlockSpec((SUBLANES, LANES), lambda i: (0, 0))],
        out_shape=[
            jax.ShapeDtypeStruct(state.shape, jnp.float32),
            jax.ShapeDtypeStruct((SUBLANES, LANES), jnp.float32),
        ],
        scratch_shapes=[pltpu.VMEM((rows, cols), jnp.float32)],
        compiler_params=pltpu.CompilerParams(vmem_limit_bytes=MIDDLE_VMEM_BYTES),
        cost_estimate=pl.CostEstimate(
            flops=10 * state.size, bytes_accessed=8 * state.size, transcendentals=0
        ),
        name="step_levels",
    )(tile, level_gain, state, low, high, weights, land_mask, sampled)
    return stepped, mark, sampled


def shard_products(index_ref, grouped_ref, error_ref, after_ref, misfit_ref, products_ref):
    del after_ref
    members = misfit_ref.shape[0]
    half_rows = SUBLANES // 2

    def lines(first):
        return jnp.concatenate(
            [grouped_ref[pl.ds(first + q, members, stride=PACK_ROWS), :] for q in range(half_rows)],
            axis=1,
        )

    grouped, misfit = lines(0), lines(half_rows)
    misfit_ref[...] = misfit
    error = jnp.concatenate(
        [error_ref[pl.ds(index_ref[0] * half_rows + q, 1), :] for q in range(half_rows)], axis=1
    )
    anomaly = grouped - jnp.sum(grouped, axis=0, keepdims=True) * (1.0 / members)
    weighted = anomaly / error
    blank = jnp.zeros((LANES - 2 * members, grouped.shape[1]), jnp.float32)
    products = lax.dot_general(
        weighted,
        jnp.concatenate([misfit, anomaly, blank], axis=0),
        (((1,), (1,)), ((), ())),
        precision=lax.Precision.HIGHEST,
        preferred_element_type=jnp.float32,
    )
    half = members // 2
    packed = jnp.concatenate(
        [products[:half, : 2 * members], products[half:, : 2 * members]], axis=1
    )
    for receiver in range(products_ref.shape[0] // half):
        products_ref[pl.ds(receiver * half, half), :] = packed


def total_of(ref, rows):
    total = ref[pl.ds(0, rows), :]
    for sender in range(1, ref.shape[0] // rows):
        total = total + ref[pl.ds(sender * rows, rows), :]
    return total


def sum_and_spread(rows, parts_ref, out_ref):
    total = total_of(parts_ref, rows)
    for receiver in range(out_ref.shape[0] // rows):
        out_ref[pl.ds(receiver * rows, rows), :] = total


def solve_and_combine(total_obs, parts_ref, grouped_ref, out_ref):
    piece = PACK_ROWS - SUBLANES
    members = out_ref.shape[0] // piece
    packed = total_of(parts_ref, members // 2)
    row = lax.broadcasted_iota(jnp.int32, (members, 2 * members), 0)
    lane = lax.broadcasted_iota(jnp.int32, (members, 2 * members), 1)
    system = jnp.concatenate([packed[:, : 2 * members], packed[:, 2 * members :]], axis=0)
    system = system / total_obs + jnp.where(row + members == lane, 1.0, 0.0)
    for k in range(members):
        at = slice(members + k, members + k + 1)
        pivot_row = system[k : k + 1, :] * (1.0 / system[k : k + 1, at])
        system = jnp.where(row == k, pivot_row, system - system[:, at] * pivot_row)
    coefficients = system[:, :members]
    combination = coefficients - jnp.sum(coefficients, axis=0, keepdims=True) * (1.0 / members)
    combination = combination + jnp.where(row == lane, 1.0, 0.0)[:, :members]
    weights = jnp.concatenate(
        [grouped_ref[pl.ds(SUBLANES + s, members, stride=PACK_ROWS), :] for s in range(piece)],
        axis=1,
    )
    combined = lax.dot_general(
        combination,
        weights,
        (((0,), (0,)), ((), ())),
        precision=lax.Precision.HIGHEST,
        preferred_element_type=jnp.float32,
    )
    for s in range(piece):
        out_ref[pl.ds(s, members, stride=piece), :] = combined[:, s * LANES : (s + 1) * LANES]


def local(kernel, name, out_shapes, *args):
    vmem = pl.BlockSpec(memory_space=pltpu.VMEM)
    smem = pl.BlockSpec(memory_space=pltpu.SMEM)
    return pl.pallas_call(
        kernel,
        in_specs=[smem if array.dtype == jnp.int32 else vmem for array in args],
        out_specs=[vmem] * len(out_shapes),
        out_shape=[jax.ShapeDtypeStruct(shape, jnp.float32) for shape in out_shapes],
        compiler_params=pltpu.CompilerParams(vmem_limit_bytes=SMALL_VMEM_BYTES),
        name=name,
    )(*args)


def swap(array, axes):
    count = lax.axis_size(axes)
    pieces = array.reshape(count, array.shape[0] // count, array.shape[1])
    moved = lax.all_to_all(pieces, axes, split_axis=0, concat_axis=0, tiled=True)
    return moved.reshape(array.shape)


def on_device(
    state,
    weights,
    land_mask,
    level_gain,
    depth,
    obs_row,
    obs_col,
    obs_quad,
    obs_frac,
    obs_value,
    obs_error,
    noise,
):
    axes = ("half", "member")
    members = lax.axis_size(axes)
    index = lax.axis_index(axes).astype(jnp.int32).reshape(1)
    tile_count = lax.axis_size("tile")
    obs_local = obs_row.shape[0]
    total_obs = obs_local * tile_count
    own = state[0]
    up = [(i, (i + 1) % tile_count) for i in range(tile_count)]
    down = [(target, source) for source, target in up]
    low = lax.ppermute(own[:, -1:], "tile", up)
    high = lax.ppermute(own[:, :1], "tile", down)
    tile = lax.axis_index("tile").astype(jnp.int32).reshape(1)
    grid = (obs_local // LANES, LANES)
    obs = (
        obs_row.reshape(grid),
        obs_col.reshape(grid),
        obs_quad.reshape(grid),
        obs_frac,
        obs_value.reshape(grid),
        noise.reshape(grid),
    )
    stepped, stepped_mark, sampled = forward(
        tile_count, tile, level_gain, depth, own, low, high, weights[0], land_mask, obs
    )
    grouped = swap(sampled, axes)
    packed_rows = members // 2
    misfit, products = local(
        shard_products,
        "shard_products",
        [(members, obs_local // members), (members * packed_rows, LANES)],
        index,
        grouped,
        obs_error.reshape(grid),
        stepped_mark,
    )
    (products,) = local(
        functools.partial(sum_and_spread, packed_rows),
        "sum_and_spread",
        [(tile_count * packed_rows, LANES)],
        swap(products, axes),
    )
    (combined,) = local(
        functools.partial(solve_and_combine, total_obs),
        "solve_and_combine",
        [(members * (PACK_ROWS - SUBLANES), LANES)],
        swap(products, "tile"),
        grouped,
    )
    tiles = swap(combined, axes)
    _, rows, cols = weights.shape
    new_weights = (
        tiles.reshape(rows // SUBLANES, cols // LANES, SUBLANES, LANES)
        .transpose(0, 2, 1, 3)
        .reshape(weights.shape)
    )
    return (stepped[None], new_weights, misfit)


def solution(mesh):
    in_specs = (
        P(("half", "member"), None, "tile", None),
        P(("half", "member"), "tile", None),
        P("tile", None),
        P(),
        P(),
        P("tile"),
        P("tile"),
        P("tile"),
        P(None, "tile"),
        P("tile"),
        P("tile"),
        P(("half", "member"), "tile"),
    )
    out_specs = (
        P(("half", "member"), None, "tile", None),
        P(("half", "member"), "tile", None),
        P(None, ("half", "member", "tile")),
    )
    return jax.shard_map(
        on_device, mesh=mesh, in_specs=in_specs, out_specs=out_specs, check_vma=False
    )
```

```python
import functools
import math

import jax
import jax.numpy as jnp
from jax import lax
from jax.experimental import pallas as pl
from jax.experimental.pallas import tpu as pltpu
from jax.sharding import PartitionSpec as P

LANES = 128
SUBLANES = 8
LEVELS_STEP = 4
OBS_STEP = 4096
GATHERED_LINES = 10
KEYS = 256
PACK_ROWS = 3 * SUBLANES
VMEM_BYTES = 60 * 1024 * 1024
MIDDLE_VMEM_BYTES = 24 * 1024 * 1024
SMALL_VMEM_BYTES = 8 * 1024 * 1024


def pick(table, index):
    return jnp.take_along_axis(table, index, axis=1, mode="promise_in_bounds")


def diffusivity_of(land, weights):
    return land.astype(jnp.float32) * (0.24 * jax.nn.sigmoid(weights))


def laplacian_of(centre, above_row, below_row):
    cols = centre.shape[1]
    sub = lax.broadcasted_iota(jnp.int32, centre.shape, 0)
    above = jnp.where(sub == 0, above_row, pltpu.roll(centre, 1, 0))
    below = jnp.where(sub == SUBLANES - 1, below_row, pltpu.roll(centre, SUBLANES - 1, 0))
    return (
        above
        + below
        + pltpu.roll(centre, 1, 1)
        + pltpu.roll(centre, cols - 1, 1)
        - 4.0 * centre
    )


def sum_column(
    gain_ref,
    depth_ref,
    state_ref,
    weights_far_ref,
    land_far_ref,
    column_ref,
    held_ref,
    flow_ref,
    weights_ref,
    land_ref,
    sems,
):
    levels, rows, cols = state_ref.shape
    parts = sems.shape[0] - 2
    per = levels // parts

    def copy(part):
        here = pl.ds(part * per, per)
        return pltpu.make_async_copy(state_ref.at[here], held_ref.at[here], sems.at[part])

    planes = [
        pltpu.make_async_copy(weights_far_ref, weights_ref, sems.at[parts]),
        pltpu.make_async_copy(land_far_ref, land_ref, sems.at[parts + 1]),
    ]
    for part in range(parts):
        copy(part).start()
    for plane in planes:
        plane.start()
    for part in range(parts):
        copy(part).wait()
        for start in range(0, rows, SUBLANES):
            here = pl.ds(start, SUBLANES)
            column = flow = None
            for level in range(part * per, (part + 1) * per):
                weighted = depth_ref[level] * held_ref[level, here, :]
                moved = gain_ref[level] * weighted
                column = weighted if column is None else column + weighted
                flow = moved if flow is None else flow + moved
            if part > 0:
                column = column + column_ref[here, :]
                flow = flow + flow_ref[here, :]
            column_ref[here, :] = column
            flow_ref[here, :] = flow
    for plane in planes:
        plane.wait()
    scale = 1.0 / math.sqrt(levels)
    blank = jnp.zeros((1, cols), jnp.float32)
    for start in range(0, rows, SUBLANES):
        here = pl.ds(start, SUBLANES)
        end = start + SUBLANES
        laplacian = laplacian_of(
            flow_ref[here, :],
            flow_ref[pl.ds(start - 1, 1), :] if start > 0 else blank,
            flow_ref[pl.ds(end, 1), :] if end < rows else blank,
        )
        diffusivity = diffusivity_of(land_ref[here, :], weights_ref[here, :])
        column_ref[here, :] = scale * (column_ref[here, :] + diffusivity * laplacian)


def has_neighbours(tile_count, tile_ref):
    tile = tile_ref[0]
    return jnp.where(tile > 0, 1.0, 0.0), jnp.where(tile < tile_count - 1, 1.0, 0.0)


def step_levels(
    tile_count, tile_ref, gain_ref, state_ref, low_ref, high_ref, weights_ref, land_ref, after_ref, stepped_ref,
    mark_ref, diffusivity_ref,
):
    del after_ref
    step = pl.program_id(0)
    levels, rows, cols = state_ref.shape
    has_low, has_high = has_neighbours(tile_count, tile_ref)

    @pl.when(step == 0)
    def _():
        diffusivity_ref[...] = diffusivity_of(land_ref[...], weights_ref[...])
        mark_ref[...] = jnp.zeros_like(mark_ref)

    for start in range(0, rows, SUBLANES):
        here = pl.ds(start, SUBLANES)
        end = start + SUBLANES
        for level in range(levels):
            centre = state_ref[level, here, :]
            laplacian = laplacian_of(
                centre,
                state_ref[level, pl.ds(start - 1, 1), :] if start > 0 else has_low * low_ref[level],
                state_ref[level, pl.ds(end, 1), :] if end < rows else has_high * high_ref[level],
            )
            factor = gain_ref[step * levels + level] * diffusivity_ref[here, :]
            stepped_ref[level, here, :] = centre + factor * laplacian


def sample_column(
    tile_count,
    tile_ref,
    gain_ref,
    depth_ref,
    column_ref,
    low_ref,
    high_ref,
    weights_ref,
    land_ref,
    row_ref,
    col_ref,
    quad_ref,
    frac_ref,
    value_ref,
    noise_ref,
    sampled_ref,
    even_ref,
    odd_ref,
    even_whole_ref,
    odd_whole_ref,
):
    rows, cols = column_ref.shape
    levels = low_ref.shape[0]
    for tile in range(rows * cols // (SUBLANES * LANES)):
        at_row, at_col = divmod(tile * LANES, cols)
        to = (tile // 2) * PACK_ROWS + (1 + tile % 2) * SUBLANES
        sampled_ref[pl.ds(to, SUBLANES), :] = weights_ref[
            pl.ds(at_row * SUBLANES, SUBLANES), pl.ds(at_col, LANES)
        ]

    def edge(ref, row, factor):
        one = pl.ds(row, 1)
        flow = jnp.zeros((1, cols), jnp.float32)
        for level in range(levels):
            flow = flow + (gain_ref[level] * depth_ref[level]) * ref[level]
        diffusivity = diffusivity_of(land_ref[one, :], weights_ref[one, :])
        return (factor / math.sqrt(levels)) * diffusivity * flow

    has_low, has_high = has_neighbours(tile_count, tile_ref)
    low, high = edge(low_ref, 0, has_low), edge(high_ref, rows - 1, has_high)
    sub = lax.broadcasted_iota(jnp.int32, (SUBLANES, LANES), 0)

    def column_tile(start, first):
        tile = column_ref[pl.ds(start, SUBLANES), pl.ds(first, LANES)]
        lanes = slice(first, first + LANES)
        if start == 0:
            tile = tile + jnp.where(sub == 0, low[:, lanes], 0.0)
        if start + SUBLANES == rows:
            tile = tile + jnp.where(sub == SUBLANES - 1, high[:, lanes], 0.0)
        return tile

    lane = lax.broadcasted_iota(jnp.int32, (SUBLANES, LANES), 1)
    doubled = (2 * lane) % LANES
    first_half = lane < LANES // 2
    for block in range(cols // (2 * LANES)):
        evens, odds = [], []
        for start in range(0, rows, SUBLANES):
            left = column_tile(start, 2 * block * LANES)
            right = column_tile(start, (2 * block + 1) * LANES)
            evens.append(jnp.where(first_half, pick(left, doubled), pick(right, doubled)))
            odds.append(
                jnp.where(first_half, pick(left, doubled + 1), pick(right, doubled + 1))
            )
        part, key = divmod(block * LANES, KEYS)
        for ref, whole_ref, pieces in (
            (even_ref, even_whole_ref, evens),
            (odd_ref, odd_whole_ref, odds),
        ):
            table = jnp.concatenate(pieces, axis=0)
            whole_ref[:, pl.ds(block * LANES, LANES)] = table
            coarse = table.astype(jnp.bfloat16)
            fine = (table - coarse.astype(jnp.float32)).astype(jnp.bfloat16)
            ref[pl.ds(2 * part * rows, rows), pl.ds(key, LANES)] = coarse
            ref[pl.ds((2 * part + 1) * rows, rows), pl.ds(key, LANES)] = fine

    count = OBS_STEP // LANES
    width = OBS_STEP - GATHERED_LINES * LANES
    keys = lax.broadcasted_iota(jnp.int16, (KEYS, width), 0)
    one, zero = jnp.bfloat16(1.0), jnp.bfloat16(0.0)
    grid_row = lax.broadcasted_iota(jnp.int32, (rows, width), 0)
    shard_rows = SUBLANES // 2

    def look_up(ref, at):
        chosen = jnp.where(keys == (at & (KEYS - 1)).astype(jnp.int16), one, zero)
        found = jnp.dot(ref[...], chosen, preferred_element_type=jnp.float32)
        result = found[:rows] + found[rows : 2 * rows]
        for part in range(1, cols // (2 * KEYS)):
            base = 2 * part * rows
            other = found[base : base + rows] + found[base + rows : base + 2 * rows]
            result = jnp.where(at // KEYS == part, other, result)
        return result

    def gather(ref, at):
        at_lane, at_block = at & (LANES - 1), at // LANES
        groups = []
        for start in range(0, rows, SUBLANES):
            here = pl.ds(start, SUBLANES)
            group = pick(ref[here, pl.ds(0, LANES)], at_lane)
            for block in range(1, cols // (2 * LANES)):
                found = pick(ref[here, pl.ds(block * LANES, LANES)], at_lane)
                group = jnp.where(at_block == block, found, group)
            groups.append(group)
        return groups

    def places(row, col, quad, second):
        row_other = row + jnp.where((quad & 1) == 1, 1, -1)
        col_other = (col + jnp.where((quad >> 1) == 1, 1, -1)) & (cols - 1)
        is_even = (col & 1) == 0
        even_at = jnp.where(is_even, col, col_other) >> 1
        odd_at = jnp.where(is_even, col_other, col) >> 1
        even_by = jnp.where(is_even, 1.0 - second, second)
        odd_by = jnp.where(is_even, second, 1.0 - second)
        return row_other, even_at, odd_at, even_by, odd_by

    def sample(i, carry):
        def put(q, predicted, perturbed):
            shard, inner = divmod(q, shard_rows)
            to = (i * (count // shard_rows) + shard) * PACK_ROWS + inner
            sampled_ref[pl.ds(to, 1), :] = predicted
            sampled_ref[pl.ds(to + shard_rows, 1), :] = perturbed - predicted

        def line(ref):
            return jnp.concatenate(
                [ref[pl.ds(i * count + q, 1), :] for q in range(GATHERED_LINES, count)], axis=1
            )

        row = line(row_ref)
        begin = i * OBS_STEP + GATHERED_LINES * LANES
        place = pl.ds(pl.multiple_of(begin, LANES), width)
        first = frac_ref[pl.ds(0, 1), place]
        second = frac_ref[pl.ds(1, 1), place]
        row_other, even_at, odd_at, even_by, odd_by = places(
            row, line(col_ref), line(quad_ref), second
        )
        along = even_by * look_up(even_ref, even_at) + odd_by * look_up(odd_ref, odd_at)
        by_row = jnp.where(
            grid_row == row, 1.0 - first, jnp.where(grid_row == row_other, first, 0.0)
        )
        predicted = jnp.sum(by_row * along, axis=0, keepdims=True)
        perturbed = line(value_ref) + line(noise_ref)
        for q in range(GATHERED_LINES, count):
            lanes = slice((q - GATHERED_LINES) * LANES, (q - GATHERED_LINES + 1) * LANES)
            put(q, predicted[:, lanes], perturbed[:, lanes])

        for q in range(GATHERED_LINES):
            here = pl.ds(i * count + q, 1)
            place = pl.ds(pl.multiple_of((i * count + q) * LANES, LANES), LANES)

            def spread(value):
                return jnp.broadcast_to(value, (SUBLANES, LANES))

            row = spread(row_ref[here, :])
            first = spread(frac_ref[pl.ds(0, 1), place])
            second = spread(frac_ref[pl.ds(1, 1), place])
            row_other, even_at, odd_at, even_by, odd_by = places(
                row, spread(col_ref[here, :]), spread(quad_ref[here, :]), second
            )
            evens, odds = gather(even_whole_ref, even_at), gather(odd_whole_ref, odd_at)
            total = jnp.zeros((SUBLANES, LANES), jnp.float32)
            for start, even, odd in zip(range(0, rows, SUBLANES), evens, odds):
                by_row = jnp.where(
                    sub == row - start, 1.0 - first, jnp.where(sub == row_other - start, first, 0.0)
                )
                total = total + by_row * (even_by * even + odd_by * odd)
            predicted = jnp.sum(total, axis=0, keepdims=True)
            put(q, predicted, value_ref[here, :] + noise_ref[here, :])
        return carry

    lax.fori_loop(0, row_ref.shape[0] // count, sample, 0)


def forward(tile_count, tile, level_gain, depth, state, low, high, weights, land_mask, obs):
    levels, rows, cols = state.shape
    per = LEVELS_STEP
    packed = (obs[0].shape[0] // (SUBLANES // 2) * PACK_ROWS, LANES)
    smem = pl.BlockSpec(memory_space=pltpu.SMEM)
    vmem = pl.BlockSpec(memory_space=pltpu.VMEM)
    plane = pl.BlockSpec((rows, cols), lambda i: (0, 0))
    halo = pl.BlockSpec((per, 1, cols), lambda i: (i, 0, 0))
    field = pl.BlockSpec((per, rows, cols), lambda i: (i, 0, 0))
    column = pl.pallas_call(
        sum_column,
        in_specs=[smem, smem] + [pl.BlockSpec(memory_space=pl.ANY)] * 3,
        out_specs=vmem,
        out_shape=jax.ShapeDtypeStruct((rows, cols), jnp.float32),
        scratch_shapes=[
            pltpu.VMEM(state.shape, jnp.float32),
            pltpu.VMEM((rows, cols), jnp.float32),
            pltpu.VMEM((rows, cols), jnp.float32),
            pltpu.VMEM((rows, cols), jnp.int32),
            pltpu.SemaphoreType.DMA((levels // per + 2,)),
        ],
        compiler_params=pltpu.CompilerParams(vmem_limit_bytes=VMEM_BYTES),
        cost_estimate=pl.CostEstimate(
            flops=6 * state.size, bytes_accessed=4 * state.size, transcendentals=0
        ),
        name="sum_column",
    )(level_gain, depth, state, weights, land_mask)
    table = pltpu.VMEM((2 * rows * cols // (2 * KEYS), KEYS), jnp.bfloat16)
    sampled = pl.pallas_call(
        functools.partial(sample_column, tile_count),
        in_specs=[smem, smem, smem] + [vmem] * (5 + len(obs)),
        out_specs=vmem,
        out_shape=jax.ShapeDtypeStruct(packed, jnp.float32),
        scratch_shapes=[table, table] + [pltpu.VMEM((rows, cols // 2), jnp.float32)] * 2,
        compiler_params=pltpu.CompilerParams(vmem_limit_bytes=MIDDLE_VMEM_BYTES),
        name="sample_column",
    )(tile, level_gain, depth, column, low, high, weights, land_mask, *obs)
    stepped, mark = pl.pallas_call(
        functools.partial(step_levels, tile_count),
        grid=(levels // per,),
        in_specs=[smem, smem, field, halo, halo, plane, plane, pl.BlockSpec(memory_space=pl.ANY)],
        out_specs=[field, pl.BlockSpec((SUBLANES, LANES), lambda i: (0, 0))],
        out_shape=[
            jax.ShapeDtypeStruct(state.shape, jnp.float32),
            jax.ShapeDtypeStruct((SUBLANES, LANES), jnp.float32),
        ],
        scratch_shapes=[pltpu.VMEM((rows, cols), jnp.float32)],
        compiler_params=pltpu.CompilerParams(vmem_limit_bytes=MIDDLE_VMEM_BYTES),
        cost_estimate=pl.CostEstimate(
            flops=10 * state.size, bytes_accessed=8 * state.size, transcendentals=0
        ),
        name="step_levels",
    )(tile, level_gain, state, low, high, weights, land_mask, sampled)
    return stepped, mark, sampled


def shard_products(index_ref, grouped_ref, error_ref, after_ref, misfit_ref, products_ref):
    del after_ref
    members = misfit_ref.shape[0]
    half_rows = SUBLANES // 2

    def lines(first):
        return jnp.concatenate(
            [grouped_ref[pl.ds(first + q, members, stride=PACK_ROWS), :] for q in range(half_rows)],
            axis=1,
        )

    grouped, misfit = lines(0), lines(half_rows)
    misfit_ref[...] = misfit
    error = jnp.concatenate(
        [error_ref[pl.ds(index_ref[0] * half_rows + q, 1), :] for q in range(half_rows)], axis=1
    )
    anomaly = grouped - jnp.sum(grouped, axis=0, keepdims=True) * (1.0 / members)
    weighted = anomaly / error
    blank = jnp.zeros((LANES - 2 * members, grouped.shape[1]), jnp.float32)
    products = lax.dot_general(
        weighted,
        jnp.concatenate([misfit, anomaly, blank], axis=0),
        (((1,), (1,)), ((), ())),
        precision=lax.Precision.HIGHEST,
        preferred_element_type=jnp.float32,
    )
    half = members // 2
    packed = jnp.concatenate(
        [products[:half, : 2 * members], products[half:, : 2 * members]], axis=1
    )
    for receiver in range(products_ref.shape[0] // half):
        products_ref[pl.ds(receiver * half, half), :] = packed


def total_of(ref, rows):
    total = ref[pl.ds(0, rows), :]
    for sender in range(1, ref.shape[0] // rows):
        total = total + ref[pl.ds(sender * rows, rows), :]
    return total


def sum_and_spread(rows, parts_ref, out_ref):
    total = total_of(parts_ref, rows)
    for receiver in range(out_ref.shape[0] // rows):
        out_ref[pl.ds(receiver * rows, rows), :] = total


def solve_and_combine(total_obs, parts_ref, grouped_ref, out_ref):
    piece = PACK_ROWS - SUBLANES
    members = out_ref.shape[0] // piece
    packed = total_of(parts_ref, members // 2)
    row = lax.broadcasted_iota(jnp.int32, (members, 2 * members), 0)
    lane = lax.broadcasted_iota(jnp.int32, (members, 2 * members), 1)
    system = jnp.concatenate([packed[:, : 2 * members], packed[:, 2 * members :]], axis=0)
    system = system / total_obs + jnp.where(row + members == lane, 1.0, 0.0)
    for k in range(members):
        at = slice(members + k, members + k + 1)
        pivot_row = system[k : k + 1, :] * (1.0 / system[k : k + 1, at])
        system = jnp.where(row == k, pivot_row, system - system[:, at] * pivot_row)
    coefficients = system[:, :members]
    combination = coefficients - jnp.sum(coefficients, axis=0, keepdims=True) * (1.0 / members)
    combination = combination + jnp.where(row == lane, 1.0, 0.0)[:, :members]
    weights = jnp.concatenate(
        [grouped_ref[pl.ds(SUBLANES + s, members, stride=PACK_ROWS), :] for s in range(piece)],
        axis=1,
    )
    combined = lax.dot_general(
        combination,
        weights,
        (((0,), (0,)), ((), ())),
        precision=lax.Precision.HIGHEST,
        preferred_element_type=jnp.float32,
    )
    for s in range(piece):
        out_ref[pl.ds(s, members, stride=piece), :] = combined[:, s * LANES : (s + 1) * LANES]


def local(kernel, name, out_shapes, *args):
    vmem = pl.BlockSpec(memory_space=pltpu.VMEM)
    smem = pl.BlockSpec(memory_space=pltpu.SMEM)
    return pl.pallas_call(
        kernel,
        in_specs=[smem if array.dtype == jnp.int32 else vmem for array in args],
        out_specs=[vmem] * len(out_shapes),
        out_shape=[jax.ShapeDtypeStruct(shape, jnp.float32) for shape in out_shapes],
        compiler_params=pltpu.CompilerParams(vmem_limit_bytes=SMALL_VMEM_BYTES),
        name=name,
    )(*args)


def swap(array, axes):
    count = lax.axis_size(axes)
    pieces = array.reshape(count, array.shape[0] // count, array.shape[1])
    moved = lax.all_to_all(pieces, axes, split_axis=0, concat_axis=0, tiled=True)
    return moved.reshape(array.shape)


def on_device(
    state,
    weights,
    land_mask,
    level_gain,
    depth,
    obs_row,
    obs_col,
    obs_quad,
    obs_frac,
    obs_value,
    obs_error,
    noise,
):
    axes = ("half", "member")
    members = lax.axis_size(axes)
    index = lax.axis_index(axes).astype(jnp.int32).reshape(1)
    tile_count = lax.axis_size("tile")
    obs_local = obs_row.shape[0]
    total_obs = obs_local * tile_count
    own = state[0]
    up = [(i, (i + 1) % tile_count) for i in range(tile_count)]
    down = [(target, source) for source, target in up]
    low = lax.ppermute(own[:, -1:], "tile", up)
    high = lax.ppermute(own[:, :1], "tile", down)
    tile = lax.axis_index("tile").astype(jnp.int32).reshape(1)
    grid = (obs_local // LANES, LANES)
    obs = (
        obs_row.reshape(grid),
        obs_col.reshape(grid),
        obs_quad.reshape(grid),
        obs_frac,
        obs_value.reshape(grid),
        noise.reshape(grid),
    )
    stepped, stepped_mark, sampled = forward(
        tile_count, tile, level_gain, depth, own, low, high, weights[0], land_mask, obs
    )
    grouped = swap(sampled, axes)
    packed_rows = members // 2
    misfit, products = local(
        shard_products,
        "shard_products",
        [(members, obs_local // members), (members * packed_rows, LANES)],
        index,
        grouped,
        obs_error.reshape(grid),
        stepped_mark,
    )
    (products,) = local(
        functools.partial(sum_and_spread, packed_rows),
        "sum_and_spread",
        [(tile_count * packed_rows, LANES)],
        swap(products, axes),
    )
    (combined,) = local(
        functools.partial(solve_and_combine, total_obs),
        "solve_and_combine",
        [(members * (PACK_ROWS - SUBLANES), LANES)],
        swap(products, "tile"),
        grouped,
    )
    tiles = swap(combined, axes)
    _, rows, cols = weights.shape
    new_weights = (
        tiles.reshape(rows // SUBLANES, cols // LANES, SUBLANES, LANES)
        .transpose(0, 2, 1, 3)
        .reshape(weights.shape)
    )
    return (stepped[None], new_weights, misfit)


def solution(mesh):
    in_specs = (
        P(("half", "member"), None, "tile", None),
        P(("half", "member"), "tile", None),
        P("tile", None),
        P(),
        P(),
        P("tile"),
        P("tile"),
        P("tile"),
        P(None, "tile"),
        P("tile"),
        P("tile"),
        P(("half", "member"), "tile"),
    )
    out_specs = (
        P(("half", "member"), None, "tile", None),
        P(("half", "member"), "tile", None),
        P(None, ("half", "member", "tile")),
    )
    return jax.shard_map(
        on_device, mesh=mesh, in_specs=in_specs, out_specs=out_specs, check_vma=False
    )
```

```python
import functools
import math

import jax
import jax.numpy as jnp
from jax import lax
from jax.experimental import pallas as pl
from jax.experimental.pallas import tpu as pltpu
from jax.sharding import PartitionSpec as P

LANES = 128
SUBLANES = 8
LEVELS_STEP = 4
OBS_STEP = 4096
GATHERED_LINES = 10
KEYS = 256
PACK_ROWS = 3 * SUBLANES
VMEM_BYTES = 60 * 1024 * 1024
MIDDLE_VMEM_BYTES = 24 * 1024 * 1024
SMALL_VMEM_BYTES = 8 * 1024 * 1024


def pick(table, index):
    return jnp.take_along_axis(table, index, axis=1, mode="promise_in_bounds")


def diffusivity_of(land, weights):
    return land.astype(jnp.float32) * (0.24 * jax.nn.sigmoid(weights))


def laplacian_of(centre, above_row, below_row):
    cols = centre.shape[1]
    sub = lax.broadcasted_iota(jnp.int32, centre.shape, 0)
    above = jnp.where(sub == 0, above_row, pltpu.roll(centre, 1, 0))
    below = jnp.where(sub == SUBLANES - 1, below_row, pltpu.roll(centre, SUBLANES - 1, 0))
    return (
        above
        + below
        + pltpu.roll(centre, 1, 1)
        + pltpu.roll(centre, cols - 1, 1)
        - 4.0 * centre
    )


def factor_place(side, levels, level):
    row, block = level % SUBLANES, side * (levels // SUBLANES) + level // SUBLANES
    return row, pl.ds(block * LANES, LANES)


def sum_column(
    tile_count,
    gain_far_ref,
    depth_far_ref,
    state_ref,
    weights_far_ref,
    land_far_ref,
    tile_far_ref,
    column_ref,
    gain_ref,
    depth_ref,
    tile_ref,
    held_ref,
    flow_ref,
    weights_ref,
    land_ref,
    sems,
):
    levels, rows, cols = state_ref.shape
    parts = sems.shape[0] - 5
    per = levels // parts

    def copy(part):
        here = pl.ds(part * per, per)
        return pltpu.make_async_copy(state_ref.at[here], held_ref.at[here], sems.at[part])

    planes = [
        pltpu.make_async_copy(weights_far_ref, weights_ref, sems.at[parts]),
        pltpu.make_async_copy(land_far_ref, land_ref, sems.at[parts + 1]),
    ]
    factors = [
        pltpu.make_async_copy(gain_far_ref, gain_ref, sems.at[parts + 2]),
        pltpu.make_async_copy(depth_far_ref, depth_ref, sems.at[parts + 3]),
        pltpu.make_async_copy(tile_far_ref, tile_ref, sems.at[parts + 4]),
    ]
    for part in range(parts):
        copy(part).start()
    for small in factors + planes:
        small.start()
    for factor in factors:
        factor.wait()
    for part in range(parts):
        copy(part).wait()
        for start in range(0, rows, SUBLANES):
            here = pl.ds(start, SUBLANES)
            column = flow = None
            for level in range(part * per, (part + 1) * per):
                weighted = depth_ref[level] * held_ref[level, here, :]
                moved = gain_ref[level] * weighted
                column = weighted if column is None else column + weighted
                flow = moved if flow is None else flow + moved
            if part > 0:
                column = column + column_ref[here, :]
                flow = flow + flow_ref[here, :]
            column_ref[here, :] = column
            flow_ref[here, :] = flow
    for plane in planes:
        plane.wait()
    scale = 1.0 / math.sqrt(levels)
    for side, has in enumerate(has_neighbours(tile_count, tile_ref)):
        for level in range(levels):
            row, lanes = factor_place(side, levels, level)
            factor = (has * scale) * (gain_ref[level] * depth_ref[level])
            column_ref[pl.ds(rows + row, 1), lanes] = jnp.full((1, LANES), factor)
    blank = jnp.zeros((1, cols), jnp.float32)
    for start in range(0, rows, SUBLANES):
        here = pl.ds(start, SUBLANES)
        end = start + SUBLANES
        laplacian = laplacian_of(
            flow_ref[here, :],
            flow_ref[pl.ds(start - 1, 1), :] if start > 0 else blank,
            flow_ref[pl.ds(end, 1), :] if end < rows else blank,
        )
        diffusivity = diffusivity_of(land_ref[here, :], weights_ref[here, :])
        column_ref[here, :] = scale * (column_ref[here, :] + diffusivity * laplacian)


def has_neighbours(tile_count, tile_ref):
    tile = tile_ref[0]
    return jnp.where(tile > 0, 1.0, 0.0), jnp.where(tile < tile_count - 1, 1.0, 0.0)


def step_levels(
    tile_count, tile_ref, gain_ref, state_ref, low_ref, high_ref, weights_ref, land_ref, after_ref, stepped_ref,
    mark_ref, diffusivity_ref,
):
    del after_ref
    step = pl.program_id(0)
    levels, rows, cols = state_ref.shape
    has_low, has_high = has_neighbours(tile_count, tile_ref)

    @pl.when(step == 0)
    def _():
        diffusivity_ref[...] = diffusivity_of(land_ref[...], weights_ref[...])
        mark_ref[...] = jnp.zeros_like(mark_ref)

    for start in range(0, rows, SUBLANES):
        here = pl.ds(start, SUBLANES)
        end = start + SUBLANES
        for level in range(levels):
            centre = state_ref[level, here, :]
            laplacian = laplacian_of(
                centre,
                state_ref[level, pl.ds(start - 1, 1), :] if start > 0 else has_low * low_ref[level],
                state_ref[level, pl.ds(end, 1), :] if end < rows else has_high * high_ref[level],
            )
            factor = gain_ref[step * levels + level] * diffusivity_ref[here, :]
            stepped_ref[level, here, :] = centre + factor * laplacian


def sample_column(
    column_ref,
    low_ref,
    high_ref,
    weights_ref,
    land_ref,
    row_ref,
    col_ref,
    quad_ref,
    frac_ref,
    value_ref,
    noise_ref,
    sampled_ref,
    even_ref,
    odd_ref,
    even_whole_ref,
    odd_whole_ref,
):
    rows, cols = weights_ref.shape
    levels = low_ref.shape[0]
    for tile in range(rows * cols // (SUBLANES * LANES)):
        at_row, at_col = divmod(tile * LANES, cols)
        to = (tile // 2) * PACK_ROWS + (1 + tile % 2) * SUBLANES
        sampled_ref[pl.ds(to, SUBLANES), :] = weights_ref[
            pl.ds(at_row * SUBLANES, SUBLANES), pl.ds(at_col, LANES)
        ]

    def edge(side, ref, row):
        one = pl.ds(row, 1)
        flow = jnp.zeros((1, cols), jnp.float32)
        for level in range(levels):
            factor_row, lanes = factor_place(side, levels, level)
            factor = column_ref[pl.ds(rows + factor_row, 1), lanes]
            flow = flow + jnp.concatenate([factor] * (cols // LANES), axis=1) * ref[level]
        return diffusivity_of(land_ref[one, :], weights_ref[one, :]) * flow

    low, high = edge(0, low_ref, 0), edge(1, high_ref, rows - 1)
    sub = lax.broadcasted_iota(jnp.int32, (SUBLANES, LANES), 0)

    def column_tile(start, first):
        tile = column_ref[pl.ds(start, SUBLANES), pl.ds(first, LANES)]
        lanes = slice(first, first + LANES)
        if start == 0:
            tile = tile + jnp.where(sub == 0, low[:, lanes], 0.0)
        if start + SUBLANES == rows:
            tile = tile + jnp.where(sub == SUBLANES - 1, high[:, lanes], 0.0)
        return tile

    lane = lax.broadcasted_iota(jnp.int32, (SUBLANES, LANES), 1)
    doubled = (2 * lane) % LANES
    first_half = lane < LANES // 2
    for block in range(cols // (2 * LANES)):
        evens, odds = [], []
        for start in range(0, rows, SUBLANES):
            left = column_tile(start, 2 * block * LANES)
            right = column_tile(start, (2 * block + 1) * LANES)
            evens.append(jnp.where(first_half, pick(left, doubled), pick(right, doubled)))
            odds.append(
                jnp.where(first_half, pick(left, doubled + 1), pick(right, doubled + 1))
            )
        part, key = divmod(block * LANES, KEYS)
        for ref, whole_ref, pieces in (
            (even_ref, even_whole_ref, evens),
            (odd_ref, odd_whole_ref, odds),
        ):
            table = jnp.concatenate(pieces, axis=0)
            whole_ref[:, pl.ds(block * LANES, LANES)] = table
            coarse = table.astype(jnp.bfloat16)
            fine = (table - coarse.astype(jnp.float32)).astype(jnp.bfloat16)
            ref[pl.ds(2 * part * rows, rows), pl.ds(key, LANES)] = coarse
            ref[pl.ds((2 * part + 1) * rows, rows), pl.ds(key, LANES)] = fine

    count = OBS_STEP // LANES
    width = OBS_STEP - GATHERED_LINES * LANES
    keys = lax.broadcasted_iota(jnp.int16, (KEYS, width), 0)
    one, zero = jnp.bfloat16(1.0), jnp.bfloat16(0.0)
    grid_row = lax.broadcasted_iota(jnp.int32, (rows, width), 0)
    shard_rows = SUBLANES // 2

    def look_up(ref, at):
        chosen = jnp.where(keys == (at & (KEYS - 1)).astype(jnp.int16), one, zero)
        found = jnp.dot(ref[...], chosen, preferred_element_type=jnp.float32)
        result = found[:rows] + found[rows : 2 * rows]
        for part in range(1, cols // (2 * KEYS)):
            base = 2 * part * rows
            other = found[base : base + rows] + found[base + rows : base + 2 * rows]
            result = jnp.where(at // KEYS == part, other, result)
        return result

    def gather(ref, at):
        at_lane, at_block = at & (LANES - 1), at // LANES
        groups = []
        for start in range(0, rows, SUBLANES):
            here = pl.ds(start, SUBLANES)
            group = pick(ref[here, pl.ds(0, LANES)], at_lane)
            for block in range(1, cols // (2 * LANES)):
                found = pick(ref[here, pl.ds(block * LANES, LANES)], at_lane)
                group = jnp.where(at_block == block, found, group)
            groups.append(group)
        return groups

    def places(row, col, quad, second):
        row_other = row + jnp.where((quad & 1) == 1, 1, -1)
        col_other = (col + jnp.where((quad >> 1) == 1, 1, -1)) & (cols - 1)
        is_even = (col & 1) == 0
        even_at = jnp.where(is_even, col, col_other) >> 1
        odd_at = jnp.where(is_even, col_other, col) >> 1
        even_by = jnp.where(is_even, 1.0 - second, second)
        odd_by = jnp.where(is_even, second, 1.0 - second)
        return row_other, even_at, odd_at, even_by, odd_by

    def sample(i, carry):
        def put(q, predicted, perturbed):
            shard, inner = divmod(q, shard_rows)
            to = (i * (count // shard_rows) + shard) * PACK_ROWS + inner
            sampled_ref[pl.ds(to, 1), :] = predicted
            sampled_ref[pl.ds(to + shard_rows, 1), :] = perturbed - predicted

        def line(ref):
            return jnp.concatenate(
                [ref[pl.ds(i * count + q, 1), :] for q in range(GATHERED_LINES, count)], axis=1
            )

        row = line(row_ref)
        begin = i * OBS_STEP + GATHERED_LINES * LANES
        place = pl.ds(pl.multiple_of(begin, LANES), width)
        first = frac_ref[pl.ds(0, 1), place]
        second = frac_ref[pl.ds(1, 1), place]
        row_other, even_at, odd_at, even_by, odd_by = places(
            row, line(col_ref), line(quad_ref), second
        )
        along = even_by * look_up(even_ref, even_at) + odd_by * look_up(odd_ref, odd_at)
        by_row = jnp.where(
            grid_row == row, 1.0 - first, jnp.where(grid_row == row_other, first, 0.0)
        )
        predicted = jnp.sum(by_row * along, axis=0, keepdims=True)
        perturbed = line(value_ref) + line(noise_ref)
        for q in range(GATHERED_LINES, count):
            lanes = slice((q - GATHERED_LINES) * LANES, (q - GATHERED_LINES + 1) * LANES)
            put(q, predicted[:, lanes], perturbed[:, lanes])

        for q in range(GATHERED_LINES):
            here = pl.ds(i * count + q, 1)
            place = pl.ds(pl.multiple_of((i * count + q) * LANES, LANES), LANES)

            def spread(value):
                return jnp.broadcast_to(value, (SUBLANES, LANES))

            row = spread(row_ref[here, :])
            first = spread(frac_ref[pl.ds(0, 1), place])
            second = spread(frac_ref[pl.ds(1, 1), place])
            row_other, even_at, odd_at, even_by, odd_by = places(
                row, spread(col_ref[here, :]), spread(quad_ref[here, :]), second
            )
            evens, odds = gather(even_whole_ref, even_at), gather(odd_whole_ref, odd_at)
            total = jnp.zeros((SUBLANES, LANES), jnp.float32)
            for start, even, odd in zip(range(0, rows, SUBLANES), evens, odds):
                by_row = jnp.where(
                    sub == row - start, 1.0 - first, jnp.where(sub == row_other - start, first, 0.0)
                )
                total = total + by_row * (even_by * even + odd_by * odd)
            predicted = jnp.sum(total, axis=0, keepdims=True)
            put(q, predicted, value_ref[here, :] + noise_ref[here, :])
        return carry

    lax.fori_loop(0, row_ref.shape[0] // count, sample, 0)


def forward(tile_count, tile, level_gain, depth, state, low, high, weights, land_mask, obs):
    levels, rows, cols = state.shape
    per = LEVELS_STEP
    packed = (obs[0].shape[0] // (SUBLANES // 2) * PACK_ROWS, LANES)
    smem = pl.BlockSpec(memory_space=pltpu.SMEM)
    vmem = pl.BlockSpec(memory_space=pltpu.VMEM)
    plane = pl.BlockSpec((rows, cols), lambda i: (0, 0))
    halo = pl.BlockSpec((per, 1, cols), lambda i: (i, 0, 0))
    field = pl.BlockSpec((per, rows, cols), lambda i: (i, 0, 0))
    column = pl.pallas_call(
        functools.partial(sum_column, tile_count),
        in_specs=[pl.BlockSpec(memory_space=pl.ANY)] * 6,
        out_specs=vmem,
        out_shape=jax.ShapeDtypeStruct((rows + SUBLANES, cols), jnp.float32),
        scratch_shapes=[
            pltpu.SMEM((levels,), jnp.float32),
            pltpu.SMEM((levels,), jnp.float32),
            pltpu.SMEM((1,), jnp.int32),
            pltpu.VMEM(state.shape, jnp.float32),
            pltpu.VMEM((rows, cols), jnp.float32),
            pltpu.VMEM((rows, cols), jnp.float32),
            pltpu.VMEM((rows, cols), jnp.int32),
            pltpu.SemaphoreType.DMA((levels // per + 5,)),
        ],
        compiler_params=pltpu.CompilerParams(vmem_limit_bytes=VMEM_BYTES),
        cost_estimate=pl.CostEstimate(
            flops=6 * state.size, bytes_accessed=4 * state.size, transcendentals=0
        ),
        name="sum_column",
    )(level_gain, depth, state, weights, land_mask, tile)
    table = pltpu.VMEM((2 * rows * cols // (2 * KEYS), KEYS), jnp.bfloat16)
    sampled = pl.pallas_call(
        sample_column,
        in_specs=[vmem] * (5 + len(obs)),
        out_specs=vmem,
        out_shape=jax.ShapeDtypeStruct(packed, jnp.float32),
        scratch_shapes=[table, table] + [pltpu.VMEM((rows, cols // 2), jnp.float32)] * 2,
        compiler_params=pltpu.CompilerParams(vmem_limit_bytes=MIDDLE_VMEM_BYTES),
        name="sample_column",
    )(column, low, high, weights, land_mask, *obs)
    stepped, mark = pl.pallas_call(
        functools.partial(step_levels, tile_count),
        grid=(levels // per,),
        in_specs=[smem, smem, field, halo, halo, plane, plane, pl.BlockSpec(memory_space=pl.ANY)],
        out_specs=[field, pl.BlockSpec((SUBLANES, LANES), lambda i: (0, 0))],
        out_shape=[
            jax.ShapeDtypeStruct(state.shape, jnp.float32),
            jax.ShapeDtypeStruct((SUBLANES, LANES), jnp.float32),
        ],
        scratch_shapes=[pltpu.VMEM((rows, cols), jnp.float32)],
        compiler_params=pltpu.CompilerParams(vmem_limit_bytes=MIDDLE_VMEM_BYTES),
        cost_estimate=pl.CostEstimate(
            flops=10 * state.size, bytes_accessed=8 * state.size, transcendentals=0
        ),
        name="step_levels",
    )(tile, level_gain, state, low, high, weights, land_mask, sampled)
    return stepped, mark, sampled


def shard_products(index_ref, grouped_ref, error_ref, after_ref, misfit_ref, products_ref):
    del after_ref
    members = misfit_ref.shape[0]
    half_rows = SUBLANES // 2

    def lines(first):
        return jnp.concatenate(
            [grouped_ref[pl.ds(first + q, members, stride=PACK_ROWS), :] for q in range(half_rows)],
            axis=1,
        )

    grouped, misfit = lines(0), lines(half_rows)
    misfit_ref[...] = misfit
    error = jnp.concatenate(
        [error_ref[pl.ds(index_ref[0] * half_rows + q, 1), :] for q in range(half_rows)], axis=1
    )
    anomaly = grouped - jnp.sum(grouped, axis=0, keepdims=True) * (1.0 / members)
    weighted = anomaly / error
    blank = jnp.zeros((LANES - 2 * members, grouped.shape[1]), jnp.float32)
    products = lax.dot_general(
        weighted,
        jnp.concatenate([misfit, anomaly, blank], axis=0),
        (((1,), (1,)), ((), ())),
        precision=lax.Precision.HIGHEST,
        preferred_element_type=jnp.float32,
    )
    half = members // 2
    packed = jnp.concatenate(
        [products[:half, : 2 * members], products[half:, : 2 * members]], axis=1
    )
    for receiver in range(products_ref.shape[0] // half):
        products_ref[pl.ds(receiver * half, half), :] = packed


def total_of(ref, rows):
    total = ref[pl.ds(0, rows), :]
    for sender in range(1, ref.shape[0] // rows):
        total = total + ref[pl.ds(sender * rows, rows), :]
    return total


def sum_and_spread(rows, parts_ref, out_ref):
    total = total_of(parts_ref, rows)
    for receiver in range(out_ref.shape[0] // rows):
        out_ref[pl.ds(receiver * rows, rows), :] = total


def solve_and_combine(total_obs, parts_ref, grouped_ref, out_ref):
    piece = PACK_ROWS - SUBLANES
    members = out_ref.shape[0] // piece
    packed = total_of(parts_ref, members // 2)
    row = lax.broadcasted_iota(jnp.int32, (members, 2 * members), 0)
    lane = lax.broadcasted_iota(jnp.int32, (members, 2 * members), 1)
    system = jnp.concatenate([packed[:, : 2 * members], packed[:, 2 * members :]], axis=0)
    system = system / total_obs + jnp.where(row + members == lane, 1.0, 0.0)
    for k in range(members):
        at = slice(members + k, members + k + 1)
        pivot_row = system[k : k + 1, :] * (1.0 / system[k : k + 1, at])
        system = jnp.where(row == k, pivot_row, system - system[:, at] * pivot_row)
    coefficients = system[:, :members]
    combination = coefficients - jnp.sum(coefficients, axis=0, keepdims=True) * (1.0 / members)
    combination = combination + jnp.where(row == lane, 1.0, 0.0)[:, :members]
    weights = jnp.concatenate(
        [grouped_ref[pl.ds(SUBLANES + s, members, stride=PACK_ROWS), :] for s in range(piece)],
        axis=1,
    )
    combined = lax.dot_general(
        combination,
        weights,
        (((0,), (0,)), ((), ())),
        precision=lax.Precision.HIGHEST,
        preferred_element_type=jnp.float32,
    )
    for s in range(piece):
        out_ref[pl.ds(s, members, stride=piece), :] = combined[:, s * LANES : (s + 1) * LANES]


def local(kernel, name, out_shapes, *args):
    vmem = pl.BlockSpec(memory_space=pltpu.VMEM)
    smem = pl.BlockSpec(memory_space=pltpu.SMEM)
    return pl.pallas_call(
        kernel,
        in_specs=[smem if array.dtype == jnp.int32 else vmem for array in args],
        out_specs=[vmem] * len(out_shapes),
        out_shape=[jax.ShapeDtypeStruct(shape, jnp.float32) for shape in out_shapes],
        compiler_params=pltpu.CompilerParams(vmem_limit_bytes=SMALL_VMEM_BYTES),
        name=name,
    )(*args)


def swap(array, axes):
    count = lax.axis_size(axes)
    pieces = array.reshape(count, array.shape[0] // count, array.shape[1])
    moved = lax.all_to_all(pieces, axes, split_axis=0, concat_axis=0, tiled=True)
    return moved.reshape(array.shape)


def on_device(
    state,
    weights,
    land_mask,
    level_gain,
    depth,
    obs_row,
    obs_col,
    obs_quad,
    obs_frac,
    obs_value,
    obs_error,
    noise,
):
    axes = ("half", "member")
    members = lax.axis_size(axes)
    index = lax.axis_index(axes).astype(jnp.int32).reshape(1)
    tile_count = lax.axis_size("tile")
    obs_local = obs_row.shape[0]
    total_obs = obs_local * tile_count
    own = state[0]
    up = [(i, (i + 1) % tile_count) for i in range(tile_count)]
    down = [(target, source) for source, target in up]
    low = lax.ppermute(own[:, -1:], "tile", up)
    high = lax.ppermute(own[:, :1], "tile", down)
    tile = lax.axis_index("tile").astype(jnp.int32).reshape(1)
    grid = (obs_local // LANES, LANES)
    obs = (
        obs_row.reshape(grid),
        obs_col.reshape(grid),
        obs_quad.reshape(grid),
        obs_frac,
        obs_value.reshape(grid),
        noise.reshape(grid),
    )
    stepped, stepped_mark, sampled = forward(
        tile_count, tile, level_gain, depth, own, low, high, weights[0], land_mask, obs
    )
    grouped = swap(sampled, axes)
    packed_rows = members // 2
    misfit, products = local(
        shard_products,
        "shard_products",
        [(members, obs_local // members), (tile_count * packed_rows, LANES)],
        index,
        grouped,
        obs_error.reshape(grid),
        stepped_mark,
    )
    (products,) = local(
        functools.partial(sum_and_spread, packed_rows),
        "sum_and_spread",
        [(members * packed_rows, LANES)],
        swap(products, "tile"),
    )
    (combined,) = local(
        functools.partial(solve_and_combine, total_obs),
        "solve_and_combine",
        [(members * (PACK_ROWS - SUBLANES), LANES)],
        swap(products, axes),
        grouped,
    )
    tiles = swap(combined, axes)
    _, rows, cols = weights.shape
    new_weights = (
        tiles.reshape(rows // SUBLANES, cols // LANES, SUBLANES, LANES)
        .transpose(0, 2, 1, 3)
        .reshape(weights.shape)
    )
    return (stepped[None], new_weights, misfit)


def solution(mesh):
    in_specs = (
        P(("half", "member"), None, "tile", None),
        P(("half", "member"), "tile", None),
        P("tile", None),
        P(),
        P(),
        P("tile"),
        P("tile"),
        P("tile"),
        P(None, "tile"),
        P("tile"),
        P("tile"),
        P(("half", "member"), "tile"),
    )
    out_specs = (
        P(("half", "member"), None, "tile", None),
        P(("half", "member"), "tile", None),
        P(None, ("half", "member", "tile")),
    )
    return jax.shard_map(
        on_device, mesh=mesh, in_specs=in_specs, out_specs=out_specs, check_vma=False
    )
```

```python
import functools
import math

import jax
import jax.numpy as jnp
from jax import lax
from jax.experimental import pallas as pl
from jax.experimental.pallas import tpu as pltpu
from jax.sharding import PartitionSpec as P

LANES = 128
SUBLANES = 8
LEVELS_STEP = 4
OBS_STEP = 4096
GATHERED_LINES = 10
KEYS = 256
PACK_ROWS = 3 * SUBLANES
VMEM_BYTES = 60 * 1024 * 1024
MIDDLE_VMEM_BYTES = 24 * 1024 * 1024
SMALL_VMEM_BYTES = 8 * 1024 * 1024


def pick(table, index):
    return jnp.take_along_axis(table, index, axis=1, mode="promise_in_bounds")


def diffusivity_of(land, weights):
    return land.astype(jnp.float32) * (0.24 * jax.nn.sigmoid(weights))


def laplacian_of(centre, above_row, below_row):
    cols = centre.shape[1]
    sub = lax.broadcasted_iota(jnp.int32, centre.shape, 0)
    above = jnp.where(sub == 0, above_row, pltpu.roll(centre, 1, 0))
    below = jnp.where(sub == SUBLANES - 1, below_row, pltpu.roll(centre, SUBLANES - 1, 0))
    return (
        above
        + below
        + pltpu.roll(centre, 1, 1)
        + pltpu.roll(centre, cols - 1, 1)
        - 4.0 * centre
    )


def factor_place(side, levels, level):
    row, block = level % SUBLANES, side * (levels // SUBLANES) + level // SUBLANES
    return row, pl.ds(block * LANES, LANES)


def sum_column(
    tile_count,
    gain_far_ref,
    depth_far_ref,
    state_ref,
    weights_far_ref,
    land_far_ref,
    tile_far_ref,
    column_ref,
    gain_ref,
    depth_ref,
    tile_ref,
    held_ref,
    flow_ref,
    weights_ref,
    land_ref,
    sems,
):
    levels, rows, cols = state_ref.shape
    parts = sems.shape[0] - 5
    per = levels // parts

    def copy(part):
        here = pl.ds(part * per, per)
        return pltpu.make_async_copy(state_ref.at[here], held_ref.at[here], sems.at[part])

    planes = [
        pltpu.make_async_copy(weights_far_ref, weights_ref, sems.at[parts]),
        pltpu.make_async_copy(land_far_ref, land_ref, sems.at[parts + 1]),
    ]
    factors = [
        pltpu.make_async_copy(gain_far_ref, gain_ref, sems.at[parts + 2]),
        pltpu.make_async_copy(depth_far_ref, depth_ref, sems.at[parts + 3]),
        pltpu.make_async_copy(tile_far_ref, tile_ref, sems.at[parts + 4]),
    ]
    for part in range(parts):
        copy(part).start()
    for small in factors + planes:
        small.start()
    for factor in factors:
        factor.wait()
    for part in range(parts):
        copy(part).wait()
        for start in range(0, rows, SUBLANES):
            here = pl.ds(start, SUBLANES)
            column = flow = None
            for level in range(part * per, (part + 1) * per):
                weighted = depth_ref[level] * held_ref[level, here, :]
                moved = gain_ref[level] * weighted
                column = weighted if column is None else column + weighted
                flow = moved if flow is None else flow + moved
            if part > 0:
                column = column + column_ref[here, :]
                flow = flow + flow_ref[here, :]
            column_ref[here, :] = column
            flow_ref[here, :] = flow
    for plane in planes:
        plane.wait()
    scale = 1.0 / math.sqrt(levels)
    for side, has in enumerate(has_neighbours(tile_count, tile_ref)):
        for level in range(levels):
            row, lanes = factor_place(side, levels, level)
            factor = (has * scale) * (gain_ref[level] * depth_ref[level])
            column_ref[pl.ds(rows + row, 1), lanes] = jnp.full((1, LANES), factor)
    blank = jnp.zeros((1, cols), jnp.float32)
    for start in range(0, rows, SUBLANES):
        here = pl.ds(start, SUBLANES)
        end = start + SUBLANES
        laplacian = laplacian_of(
            flow_ref[here, :],
            flow_ref[pl.ds(start - 1, 1), :] if start > 0 else blank,
            flow_ref[pl.ds(end, 1), :] if end < rows else blank,
        )
        diffusivity = diffusivity_of(land_ref[here, :], weights_ref[here, :])
        column_ref[here, :] = scale * (column_ref[here, :] + diffusivity * laplacian)


def has_neighbours(tile_count, tile_ref):
    tile = tile_ref[0]
    return jnp.where(tile > 0, 1.0, 0.0), jnp.where(tile < tile_count - 1, 1.0, 0.0)


def step_levels(
    tile_count, tile_ref, gain_ref, state_ref, low_ref, high_ref, weights_ref, land_ref, after_ref, stepped_ref,
    mark_ref, diffusivity_ref,
):
    del after_ref
    step = pl.program_id(0)
    levels, rows, cols = state_ref.shape
    has_low, has_high = has_neighbours(tile_count, tile_ref)

    @pl.when(step == 0)
    def _():
        diffusivity_ref[...] = diffusivity_of(land_ref[...], weights_ref[...])
        mark_ref[...] = jnp.zeros_like(mark_ref)

    for start in range(0, rows, SUBLANES):
        here = pl.ds(start, SUBLANES)
        end = start + SUBLANES
        for level in range(levels):
            centre = state_ref[level, here, :]
            laplacian = laplacian_of(
                centre,
                state_ref[level, pl.ds(start - 1, 1), :] if start > 0 else has_low * low_ref[level],
                state_ref[level, pl.ds(end, 1), :] if end < rows else has_high * high_ref[level],
            )
            factor = gain_ref[step * levels + level] * diffusivity_ref[here, :]
            stepped_ref[level, here, :] = centre + factor * laplacian


def sample_column(
    column_ref,
    low_ref,
    high_ref,
    weights_ref,
    land_ref,
    row_ref,
    col_ref,
    quad_ref,
    frac_ref,
    value_ref,
    noise_ref,
    sampled_ref,
    even_ref,
    odd_ref,
    even_whole_ref,
    odd_whole_ref,
):
    rows, cols = weights_ref.shape
    levels = low_ref.shape[0]
    for tile in range(rows * cols // (SUBLANES * LANES)):
        at_row, at_col = divmod(tile * LANES, cols)
        to = (tile // 2) * PACK_ROWS + (1 + tile % 2) * SUBLANES
        sampled_ref[pl.ds(to, SUBLANES), :] = weights_ref[
            pl.ds(at_row * SUBLANES, SUBLANES), pl.ds(at_col, LANES)
        ]

    def edge(side, ref, row):
        one = pl.ds(row, 1)
        flow = jnp.zeros((1, cols), jnp.float32)
        for level in range(levels):
            factor_row, lanes = factor_place(side, levels, level)
            factor = column_ref[pl.ds(rows + factor_row, 1), lanes]
            flow = flow + jnp.concatenate([factor] * (cols // LANES), axis=1) * ref[level]
        return diffusivity_of(land_ref[one, :], weights_ref[one, :]) * flow

    low, high = edge(0, low_ref, 0), edge(1, high_ref, rows - 1)
    sub = lax.broadcasted_iota(jnp.int32, (SUBLANES, LANES), 0)

    def column_tile(start, first):
        tile = column_ref[pl.ds(start, SUBLANES), pl.ds(first, LANES)]
        lanes = slice(first, first + LANES)
        if start == 0:
            tile = tile + jnp.where(sub == 0, low[:, lanes], 0.0)
        if start + SUBLANES == rows:
            tile = tile + jnp.where(sub == SUBLANES - 1, high[:, lanes], 0.0)
        return tile

    lane = lax.broadcasted_iota(jnp.int32, (SUBLANES, LANES), 1)
    doubled = (2 * lane) % LANES
    first_half = lane < LANES // 2
    for block in range(cols // (2 * LANES)):
        evens, odds = [], []
        for start in range(0, rows, SUBLANES):
            left = column_tile(start, 2 * block * LANES)
            right = column_tile(start, (2 * block + 1) * LANES)
            evens.append(jnp.where(first_half, pick(left, doubled), pick(right, doubled)))
            odds.append(
                jnp.where(first_half, pick(left, doubled + 1), pick(right, doubled + 1))
            )
        part, key = divmod(block * LANES, KEYS)
        for ref, whole_ref, pieces in (
            (even_ref, even_whole_ref, evens),
            (odd_ref, odd_whole_ref, odds),
        ):
            table = jnp.concatenate(pieces, axis=0)
            whole_ref[:, pl.ds(block * LANES, LANES)] = table
            coarse = table.astype(jnp.bfloat16)
            fine = (table - coarse.astype(jnp.float32)).astype(jnp.bfloat16)
            ref[pl.ds(2 * part * rows, rows), pl.ds(key, LANES)] = coarse
            ref[pl.ds((2 * part + 1) * rows, rows), pl.ds(key, LANES)] = fine

    count = OBS_STEP // LANES
    width = OBS_STEP - GATHERED_LINES * LANES
    keys = lax.broadcasted_iota(jnp.int16, (KEYS, width), 0)
    one, zero = jnp.bfloat16(1.0), jnp.bfloat16(0.0)
    grid_row = lax.broadcasted_iota(jnp.int32, (rows, width), 0)
    shard_rows = SUBLANES // 2

    def look_up(ref, at):
        chosen = jnp.where(keys == (at & (KEYS - 1)).astype(jnp.int16), one, zero)
        found = jnp.dot(ref[...], chosen, preferred_element_type=jnp.float32)
        result = found[:rows] + found[rows : 2 * rows]
        for part in range(1, cols // (2 * KEYS)):
            base = 2 * part * rows
            other = found[base : base + rows] + found[base + rows : base + 2 * rows]
            result = jnp.where(at // KEYS == part, other, result)
        return result

    def gather(ref, at):
        at_lane, at_block = at & (LANES - 1), at // LANES
        groups = []
        for start in range(0, rows, SUBLANES):
            here = pl.ds(start, SUBLANES)
            group = pick(ref[here, pl.ds(0, LANES)], at_lane)
            for block in range(1, cols // (2 * LANES)):
                found = pick(ref[here, pl.ds(block * LANES, LANES)], at_lane)
                group = jnp.where(at_block == block, found, group)
            groups.append(group)
        return groups

    def places(row, col, quad, second):
        row_other = row + jnp.where((quad & 1) == 1, 1, -1)
        col_other = (col + jnp.where((quad >> 1) == 1, 1, -1)) & (cols - 1)
        is_even = (col & 1) == 0
        even_at = jnp.where(is_even, col, col_other) >> 1
        odd_at = jnp.where(is_even, col_other, col) >> 1
        even_by = jnp.where(is_even, 1.0 - second, second)
        odd_by = jnp.where(is_even, second, 1.0 - second)
        return row_other, even_at, odd_at, even_by, odd_by

    def sample(i, carry):
        def put(q, predicted, perturbed):
            shard, inner = divmod(q, shard_rows)
            to = (i * (count // shard_rows) + shard) * PACK_ROWS + inner
            sampled_ref[pl.ds(to, 1), :] = predicted
            sampled_ref[pl.ds(to + shard_rows, 1), :] = perturbed - predicted

        def line(ref):
            return jnp.concatenate(
                [ref[pl.ds(i * count + q, 1), :] for q in range(GATHERED_LINES, count)], axis=1
            )

        row = line(row_ref)
        begin = i * OBS_STEP + GATHERED_LINES * LANES
        place = pl.ds(pl.multiple_of(begin, LANES), width)
        first = frac_ref[pl.ds(0, 1), place]
        second = frac_ref[pl.ds(1, 1), place]
        row_other, even_at, odd_at, even_by, odd_by = places(
            row, line(col_ref), line(quad_ref), second
        )
        along = even_by * look_up(even_ref, even_at) + odd_by * look_up(odd_ref, odd_at)
        by_row = jnp.where(
            grid_row == row, 1.0 - first, jnp.where(grid_row == row_other, first, 0.0)
        )
        predicted = jnp.sum(by_row * along, axis=0, keepdims=True)
        perturbed = line(value_ref) + line(noise_ref)
        for q in range(GATHERED_LINES, count):
            lanes = slice((q - GATHERED_LINES) * LANES, (q - GATHERED_LINES + 1) * LANES)
            put(q, predicted[:, lanes], perturbed[:, lanes])

        for q in range(GATHERED_LINES):
            here = pl.ds(i * count + q, 1)
            place = pl.ds(pl.multiple_of((i * count + q) * LANES, LANES), LANES)

            def spread(value):
                return jnp.broadcast_to(value, (SUBLANES, LANES))

            row = spread(row_ref[here, :])
            first = spread(frac_ref[pl.ds(0, 1), place])
            second = spread(frac_ref[pl.ds(1, 1), place])
            row_other, even_at, odd_at, even_by, odd_by = places(
                row, spread(col_ref[here, :]), spread(quad_ref[here, :]), second
            )
            evens, odds = gather(even_whole_ref, even_at), gather(odd_whole_ref, odd_at)
            total = jnp.zeros((SUBLANES, LANES), jnp.float32)
            for start, even, odd in zip(range(0, rows, SUBLANES), evens, odds):
                by_row = jnp.where(
                    sub == row - start, 1.0 - first, jnp.where(sub == row_other - start, first, 0.0)
                )
                total = total + by_row * (even_by * even + odd_by * odd)
            predicted = jnp.sum(total, axis=0, keepdims=True)
            put(q, predicted, value_ref[here, :] + noise_ref[here, :])
        return carry

    lax.fori_loop(0, row_ref.shape[0] // count, sample, 0)


def forward(tile_count, tile, level_gain, depth, state, low, high, weights, land_mask, obs):
    levels, rows, cols = state.shape
    per = LEVELS_STEP
    packed = (obs[0].shape[0] // (SUBLANES // 2) * PACK_ROWS, LANES)
    smem = pl.BlockSpec(memory_space=pltpu.SMEM)
    vmem = pl.BlockSpec(memory_space=pltpu.VMEM)
    plane = pl.BlockSpec((rows, cols), lambda i: (0, 0))
    halo = pl.BlockSpec((per, 1, cols), lambda i: (i, 0, 0))
    field = pl.BlockSpec((per, rows, cols), lambda i: (i, 0, 0))
    column = pl.pallas_call(
        functools.partial(sum_column, tile_count),
        in_specs=[pl.BlockSpec(memory_space=pl.ANY)] * 6,
        out_specs=vmem,
        out_shape=jax.ShapeDtypeStruct((rows + SUBLANES, cols), jnp.float32),
        scratch_shapes=[
            pltpu.SMEM((levels,), jnp.float32),
            pltpu.SMEM((levels,), jnp.float32),
            pltpu.SMEM((1,), jnp.int32),
            pltpu.VMEM(state.shape, jnp.float32),
            pltpu.VMEM((rows, cols), jnp.float32),
            pltpu.VMEM((rows, cols), jnp.float32),
            pltpu.VMEM((rows, cols), jnp.int32),
            pltpu.SemaphoreType.DMA((levels // per + 5,)),
        ],
        compiler_params=pltpu.CompilerParams(vmem_limit_bytes=VMEM_BYTES),
        cost_estimate=pl.CostEstimate(
            flops=6 * state.size, bytes_accessed=4 * state.size, transcendentals=0
        ),
        name="sum_column",
    )(level_gain, depth, state, weights, land_mask, tile)
    table = pltpu.VMEM((2 * rows * cols // (2 * KEYS), KEYS), jnp.bfloat16)
    sampled = pl.pallas_call(
        sample_column,
        in_specs=[vmem] * (5 + len(obs)),
        out_specs=vmem,
        out_shape=jax.ShapeDtypeStruct(packed, jnp.float32),
        scratch_shapes=[table, table] + [pltpu.VMEM((rows, cols // 2), jnp.float32)] * 2,
        compiler_params=pltpu.CompilerParams(vmem_limit_bytes=MIDDLE_VMEM_BYTES),
        name="sample_column",
    )(column, low, high, weights, land_mask, *obs)
    stepped, mark = pl.pallas_call(
        functools.partial(step_levels, tile_count),
        grid=(levels // per,),
        in_specs=[smem, smem, field, halo, halo, plane, plane, pl.BlockSpec(memory_space=pl.ANY)],
        out_specs=[field, pl.BlockSpec((SUBLANES, LANES), lambda i: (0, 0))],
        out_shape=[
            jax.ShapeDtypeStruct(state.shape, jnp.float32),
            jax.ShapeDtypeStruct((SUBLANES, LANES), jnp.float32),
        ],
        scratch_shapes=[pltpu.VMEM((rows, cols), jnp.float32)],
        compiler_params=pltpu.CompilerParams(vmem_limit_bytes=MIDDLE_VMEM_BYTES),
        cost_estimate=pl.CostEstimate(
            flops=10 * state.size, bytes_accessed=8 * state.size, transcendentals=0
        ),
        name="step_levels",
    )(tile, level_gain, state, low, high, weights, land_mask, sampled)
    return stepped, mark, sampled


def shard_products(index_ref, grouped_ref, error_ref, after_ref, misfit_ref, products_ref):
    del after_ref
    members = misfit_ref.shape[0]
    half_rows = SUBLANES // 2

    def lines(first):
        return jnp.concatenate(
            [grouped_ref[pl.ds(first + q, members, stride=PACK_ROWS), :] for q in range(half_rows)],
            axis=1,
        )

    grouped, misfit = lines(0), lines(half_rows)
    misfit_ref[...] = misfit
    error = jnp.concatenate(
        [error_ref[pl.ds(index_ref[0] * half_rows + q, 1), :] for q in range(half_rows)], axis=1
    )
    anomaly = grouped - jnp.sum(grouped, axis=0, keepdims=True) * (1.0 / members)
    weighted = anomaly / error
    blank = jnp.zeros((LANES - 2 * members, grouped.shape[1]), jnp.float32)
    products = lax.dot_general(
        weighted,
        jnp.concatenate([misfit, anomaly, blank], axis=0),
        (((1,), (1,)), ((), ())),
        precision=lax.Precision.HIGHEST,
        preferred_element_type=jnp.float32,
    )
    half = members // 2
    packed = jnp.concatenate(
        [products[:half, : 2 * members], products[half:, : 2 * members]], axis=1
    )
    for receiver in range(products_ref.shape[0] // half):
        products_ref[pl.ds(receiver * half, half), :] = packed


def total_of(ref, rows):
    total = ref[pl.ds(0, rows), :]
    for sender in range(1, ref.shape[0] // rows):
        total = total + ref[pl.ds(sender * rows, rows), :]
    return total


def sum_and_spread(rows, parts_ref, out_ref):
    total = total_of(parts_ref, rows)
    for receiver in range(out_ref.shape[0] // rows):
        out_ref[pl.ds(receiver * rows, rows), :] = total


def solve_and_combine(total_obs, parts_ref, grouped_ref, out_ref):
    piece = PACK_ROWS - SUBLANES
    members = out_ref.shape[0] // piece
    packed = total_of(parts_ref, members // 2)
    row = lax.broadcasted_iota(jnp.int32, (members, 2 * members), 0)
    lane = lax.broadcasted_iota(jnp.int32, (members, 2 * members), 1)
    system = jnp.concatenate([packed[:, : 2 * members], packed[:, 2 * members :]], axis=0)
    system = system / total_obs + jnp.where(row + members == lane, 1.0, 0.0)
    for k in range(0, members, 2):
        at, at_next = (slice(members + i, members + i + 1) for i in (k, k + 1))
        left = jnp.broadcast_to(system[:, at], system.shape)
        right = jnp.broadcast_to(system[:, at_next], system.shape)
        first, second = system[k : k + 1, :], system[k + 1 : k + 2, :]
        a, b = left[k : k + 1, :], right[k : k + 1, :]
        c, d = left[k + 1 : k + 2, :], right[k + 1 : k + 2, :]
        scale = 1.0 / (a * d - b * c)
        pivot = (d * first - b * second) * scale
        pivot_next = (a * second - c * first) * scale
        others = system - left * pivot - right * pivot_next
        system = jnp.where(row == k, pivot, jnp.where(row == k + 1, pivot_next, others))
    coefficients = system[:, :members]
    combination = coefficients - jnp.sum(coefficients, axis=0, keepdims=True) * (1.0 / members)
    combination = combination + jnp.where(row == lane, 1.0, 0.0)[:, :members]
    weights = jnp.concatenate(
        [grouped_ref[pl.ds(SUBLANES + s, members, stride=PACK_ROWS), :] for s in range(piece)],
        axis=1,
    )
    combined = lax.dot_general(
        combination,
        weights,
        (((0,), (0,)), ((), ())),
        precision=lax.Precision.HIGHEST,
        preferred_element_type=jnp.float32,
    )
    for s in range(piece):
        out_ref[pl.ds(s, members, stride=piece), :] = combined[:, s * LANES : (s + 1) * LANES]


def local(kernel, name, out_shapes, *args):
    vmem = pl.BlockSpec(memory_space=pltpu.VMEM)
    smem = pl.BlockSpec(memory_space=pltpu.SMEM)
    return pl.pallas_call(
        kernel,
        in_specs=[smem if array.dtype == jnp.int32 else vmem for array in args],
        out_specs=[vmem] * len(out_shapes),
        out_shape=[jax.ShapeDtypeStruct(shape, jnp.float32) for shape in out_shapes],
        compiler_params=pltpu.CompilerParams(vmem_limit_bytes=SMALL_VMEM_BYTES),
        name=name,
    )(*args)


def swap(array, axes):
    count = lax.axis_size(axes)
    pieces = array.reshape(count, array.shape[0] // count, array.shape[1])
    moved = lax.all_to_all(pieces, axes, split_axis=0, concat_axis=0, tiled=True)
    return moved.reshape(array.shape)


def on_device(
    state,
    weights,
    land_mask,
    level_gain,
    depth,
    obs_row,
    obs_col,
    obs_quad,
    obs_frac,
    obs_value,
    obs_error,
    noise,
):
    axes = ("half", "member")
    members = lax.axis_size(axes)
    index = lax.axis_index(axes).astype(jnp.int32).reshape(1)
    tile_count = lax.axis_size("tile")
    obs_local = obs_row.shape[0]
    total_obs = obs_local * tile_count
    own = state[0]
    up = [(i, (i + 1) % tile_count) for i in range(tile_count)]
    down = [(target, source) for source, target in up]
    low = lax.ppermute(own[:, -1:], "tile", up)
    high = lax.ppermute(own[:, :1], "tile", down)
    tile = lax.axis_index("tile").astype(jnp.int32).reshape(1)
    grid = (obs_local // LANES, LANES)
    obs = (
        obs_row.reshape(grid),
        obs_col.reshape(grid),
        obs_quad.reshape(grid),
        obs_frac,
        obs_value.reshape(grid),
        noise.reshape(grid),
    )
    stepped, stepped_mark, sampled = forward(
        tile_count, tile, level_gain, depth, own, low, high, weights[0], land_mask, obs
    )
    grouped = swap(sampled, axes)
    packed_rows = members // 2
    misfit, products = local(
        shard_products,
        "shard_products",
        [(members, obs_local // members), (tile_count * packed_rows, LANES)],
        index,
        grouped,
        obs_error.reshape(grid),
        stepped_mark,
    )
    (products,) = local(
        functools.partial(sum_and_spread, packed_rows),
        "sum_and_spread",
        [(members * packed_rows, LANES)],
        swap(products, "tile"),
    )
    (combined,) = local(
        functools.partial(solve_and_combine, total_obs),
        "solve_and_combine",
        [(members * (PACK_ROWS - SUBLANES), LANES)],
        swap(products, axes),
        grouped,
    )
    tiles = swap(combined, axes)
    _, rows, cols = weights.shape
    new_weights = (
        tiles.reshape(rows // SUBLANES, cols // LANES, SUBLANES, LANES)
        .transpose(0, 2, 1, 3)
        .reshape(weights.shape)
    )
    return (stepped[None], new_weights, misfit)


def solution(mesh):
    in_specs = (
        P(("half", "member"), None, "tile", None),
        P(("half", "member"), "tile", None),
        P("tile", None),
        P(),
        P(),
        P("tile"),
        P("tile"),
        P("tile"),
        P(None, "tile"),
        P("tile"),
        P("tile"),
        P(("half", "member"), "tile"),
    )
    out_specs = (
        P(("half", "member"), None, "tile", None),
        P(("half", "member"), "tile", None),
        P(None, ("half", "member", "tile")),
    )
    return jax.shard_map(
        on_device, mesh=mesh, in_specs=in_specs, out_specs=out_specs, check_vma=False
    )
```

```python
import functools
import math

import jax
import jax.numpy as jnp
from jax import lax
from jax.experimental import pallas as pl
from jax.experimental.pallas import tpu as pltpu
from jax.sharding import PartitionSpec as P

LANES = 128
SUBLANES = 8
LEVELS_STEP = 4
OBS_STEP = 4096
GATHERED_LINES = 10
KEYS = 256
PACK_ROWS = 3 * SUBLANES
VMEM_BYTES = 60 * 1024 * 1024
MIDDLE_VMEM_BYTES = 24 * 1024 * 1024
SMALL_VMEM_BYTES = 8 * 1024 * 1024


def pick(table, index):
    return jnp.take_along_axis(table, index, axis=1, mode="promise_in_bounds")


def diffusivity_of(land, weights):
    return land.astype(jnp.float32) * (0.24 * jax.nn.sigmoid(weights))


def laplacian_of(centre, above_row, below_row):
    cols = centre.shape[1]
    sub = lax.broadcasted_iota(jnp.int32, centre.shape, 0)
    above = jnp.where(sub == 0, above_row, pltpu.roll(centre, 1, 0))
    below = jnp.where(sub == SUBLANES - 1, below_row, pltpu.roll(centre, SUBLANES - 1, 0))
    return (
        above
        + below
        + pltpu.roll(centre, 1, 1)
        + pltpu.roll(centre, cols - 1, 1)
        - 4.0 * centre
    )


def factor_place(side, levels, level):
    row, block = level % SUBLANES, side * (levels // SUBLANES) + level // SUBLANES
    return row, pl.ds(block * LANES, LANES)


def sum_column(
    tile_count,
    gain_far_ref,
    depth_far_ref,
    state_ref,
    weights_far_ref,
    land_far_ref,
    tile_far_ref,
    column_ref,
    gain_ref,
    depth_ref,
    tile_ref,
    held_ref,
    flow_ref,
    weights_ref,
    land_ref,
    sems,
):
    levels, rows, cols = state_ref.shape
    parts = sems.shape[0] - 5
    per = levels // parts

    def copy(part):
        here = pl.ds(part * per, per)
        return pltpu.make_async_copy(state_ref.at[here], held_ref.at[here], sems.at[part])

    planes = [
        pltpu.make_async_copy(weights_far_ref, weights_ref, sems.at[parts]),
        pltpu.make_async_copy(land_far_ref, land_ref, sems.at[parts + 1]),
    ]
    factors = [
        pltpu.make_async_copy(gain_far_ref, gain_ref, sems.at[parts + 2]),
        pltpu.make_async_copy(depth_far_ref, depth_ref, sems.at[parts + 3]),
        pltpu.make_async_copy(tile_far_ref, tile_ref, sems.at[parts + 4]),
    ]
    for part in range(parts):
        copy(part).start()
    for small in factors + planes:
        small.start()
    for factor in factors:
        factor.wait()
    for part in range(parts):
        copy(part).wait()
        for start in range(0, rows, SUBLANES):
            here = pl.ds(start, SUBLANES)
            column = flow = None
            for level in range(part * per, (part + 1) * per):
                weighted = depth_ref[level] * held_ref[level, here, :]
                moved = gain_ref[level] * weighted
                column = weighted if column is None else column + weighted
                flow = moved if flow is None else flow + moved
            if part > 0:
                column = column + column_ref[here, :]
                flow = flow + flow_ref[here, :]
            column_ref[here, :] = column
            flow_ref[here, :] = flow
    for plane in planes:
        plane.wait()
    scale = 1.0 / math.sqrt(levels)
    for side, has in enumerate(has_neighbours(tile_count, tile_ref)):
        for level in range(levels):
            row, lanes = factor_place(side, levels, level)
            factor = (has * scale) * (gain_ref[level] * depth_ref[level])
            column_ref[pl.ds(rows + row, 1), lanes] = jnp.full((1, LANES), factor)
    blank = jnp.zeros((1, cols), jnp.float32)
    for start in range(0, rows, SUBLANES):
        here = pl.ds(start, SUBLANES)
        end = start + SUBLANES
        laplacian = laplacian_of(
            flow_ref[here, :],
            flow_ref[pl.ds(start - 1, 1), :] if start > 0 else blank,
            flow_ref[pl.ds(end, 1), :] if end < rows else blank,
        )
        diffusivity = diffusivity_of(land_ref[here, :], weights_ref[here, :])
        column_ref[here, :] = scale * (column_ref[here, :] + diffusivity * laplacian)


def has_neighbours(tile_count, tile_ref):
    tile = tile_ref[0]
    return jnp.where(tile > 0, 1.0, 0.0), jnp.where(tile < tile_count - 1, 1.0, 0.0)


def step_levels(
    tile_count, tile_ref, gain_ref, state_ref, low_ref, high_ref, weights_ref, land_ref, after_ref, stepped_ref,
    mark_ref, diffusivity_ref,
):
    del after_ref
    step = pl.program_id(0)
    levels, rows, cols = state_ref.shape
    has_low, has_high = has_neighbours(tile_count, tile_ref)

    @pl.when(step == 0)
    def _():
        diffusivity_ref[...] = diffusivity_of(land_ref[...], weights_ref[...])
        mark_ref[...] = jnp.zeros_like(mark_ref)

    for start in range(0, rows, SUBLANES):
        here = pl.ds(start, SUBLANES)
        end = start + SUBLANES
        for level in range(levels):
            centre = state_ref[level, here, :]
            laplacian = laplacian_of(
                centre,
                state_ref[level, pl.ds(start - 1, 1), :] if start > 0 else has_low * low_ref[level],
                state_ref[level, pl.ds(end, 1), :] if end < rows else has_high * high_ref[level],
            )
            factor = gain_ref[step * levels + level] * diffusivity_ref[here, :]
            stepped_ref[level, here, :] = centre + factor * laplacian


def sample_column(
    column_ref,
    low_ref,
    high_ref,
    weights_ref,
    land_ref,
    row_ref,
    col_ref,
    quad_ref,
    frac_ref,
    value_ref,
    noise_ref,
    sampled_ref,
    even_ref,
    odd_ref,
    even_whole_ref,
    odd_whole_ref,
):
    rows, cols = weights_ref.shape
    levels = low_ref.shape[0]
    for tile in range(rows * cols // (SUBLANES * LANES)):
        at_row, at_col = divmod(tile * LANES, cols)
        to = (tile // 2) * PACK_ROWS + (1 + tile % 2) * SUBLANES
        sampled_ref[pl.ds(to, SUBLANES), :] = weights_ref[
            pl.ds(at_row * SUBLANES, SUBLANES), pl.ds(at_col, LANES)
        ]

    def edge(side, ref, row):
        one = pl.ds(row, 1)
        flow = jnp.zeros((1, cols), jnp.float32)
        for level in range(levels):
            factor_row, lanes = factor_place(side, levels, level)
            factor = column_ref[pl.ds(rows + factor_row, 1), lanes]
            flow = flow + jnp.concatenate([factor] * (cols // LANES), axis=1) * ref[level]
        return diffusivity_of(land_ref[one, :], weights_ref[one, :]) * flow

    low, high = edge(0, low_ref, 0), edge(1, high_ref, rows - 1)
    sub = lax.broadcasted_iota(jnp.int32, (SUBLANES, LANES), 0)

    def column_tile(start, first):
        tile = column_ref[pl.ds(start, SUBLANES), pl.ds(first, LANES)]
        lanes = slice(first, first + LANES)
        if start == 0:
            tile = tile + jnp.where(sub == 0, low[:, lanes], 0.0)
        if start + SUBLANES == rows:
            tile = tile + jnp.where(sub == SUBLANES - 1, high[:, lanes], 0.0)
        return tile

    lane = lax.broadcasted_iota(jnp.int32, (SUBLANES, LANES), 1)
    doubled = (2 * lane) % LANES
    first_half = lane < LANES // 2
    for block in range(cols // (2 * LANES)):
        evens, odds = [], []
        for start in range(0, rows, SUBLANES):
            left = column_tile(start, 2 * block * LANES)
            right = column_tile(start, (2 * block + 1) * LANES)
            evens.append(jnp.where(first_half, pick(left, doubled), pick(right, doubled)))
            odds.append(
                jnp.where(first_half, pick(left, doubled + 1), pick(right, doubled + 1))
            )
        part, key = divmod(block * LANES, KEYS)
        for ref, whole_ref, pieces in (
            (even_ref, even_whole_ref, evens),
            (odd_ref, odd_whole_ref, odds),
        ):
            table = jnp.concatenate(pieces, axis=0)
            whole_ref[:, pl.ds(block * LANES, LANES)] = table
            coarse = table.astype(jnp.bfloat16)
            fine = (table - coarse.astype(jnp.float32)).astype(jnp.bfloat16)
            ref[pl.ds(2 * part * rows, rows), pl.ds(key, LANES)] = coarse
            ref[pl.ds((2 * part + 1) * rows, rows), pl.ds(key, LANES)] = fine

    count = OBS_STEP // LANES
    width = OBS_STEP - GATHERED_LINES * LANES
    keys = lax.broadcasted_iota(jnp.int16, (KEYS, width), 0)
    one, zero = jnp.bfloat16(1.0), jnp.bfloat16(0.0)
    grid_row = lax.broadcasted_iota(jnp.int32, (rows, width), 0)
    shard_rows = SUBLANES // 2

    def look_up(ref, at):
        chosen = jnp.where(keys == (at & (KEYS - 1)).astype(jnp.int16), one, zero)
        found = jnp.dot(ref[...], chosen, preferred_element_type=jnp.float32)
        result = found[:rows] + found[rows : 2 * rows]
        for part in range(1, cols // (2 * KEYS)):
            base = 2 * part * rows
            other = found[base : base + rows] + found[base + rows : base + 2 * rows]
            result = jnp.where(at // KEYS == part, other, result)
        return result

    def gather(ref, at):
        at_lane, at_block = at & (LANES - 1), at // LANES
        groups = []
        for start in range(0, rows, SUBLANES):
            here = pl.ds(start, SUBLANES)
            group = pick(ref[here, pl.ds(0, LANES)], at_lane)
            for block in range(1, cols // (2 * LANES)):
                found = pick(ref[here, pl.ds(block * LANES, LANES)], at_lane)
                group = jnp.where(at_block == block, found, group)
            groups.append(group)
        return groups

    def places(row, col, quad, second):
        row_other = row + jnp.where((quad & 1) == 1, 1, -1)
        col_other = (col + jnp.where((quad >> 1) == 1, 1, -1)) & (cols - 1)
        is_even = (col & 1) == 0
        even_at = jnp.where(is_even, col, col_other) >> 1
        odd_at = jnp.where(is_even, col_other, col) >> 1
        even_by = jnp.where(is_even, 1.0 - second, second)
        odd_by = jnp.where(is_even, second, 1.0 - second)
        return row_other, even_at, odd_at, even_by, odd_by

    def sample(i, carry):
        def put(q, predicted, perturbed):
            shard, inner = divmod(q, shard_rows)
            to = (i * (count // shard_rows) + shard) * PACK_ROWS + inner
            sampled_ref[pl.ds(to, 1), :] = predicted
            sampled_ref[pl.ds(to + shard_rows, 1), :] = perturbed - predicted

        def line(ref):
            return jnp.concatenate(
                [ref[pl.ds(i * count + q, 1), :] for q in range(GATHERED_LINES, count)], axis=1
            )

        row = line(row_ref)
        begin = i * OBS_STEP + GATHERED_LINES * LANES
        place = pl.ds(pl.multiple_of(begin, LANES), width)
        first = frac_ref[pl.ds(0, 1), place]
        second = frac_ref[pl.ds(1, 1), place]
        row_other, even_at, odd_at, even_by, odd_by = places(
            row, line(col_ref), line(quad_ref), second
        )
        along = even_by * look_up(even_ref, even_at) + odd_by * look_up(odd_ref, odd_at)
        by_row = jnp.where(
            grid_row == row, 1.0 - first, jnp.where(grid_row == row_other, first, 0.0)
        )
        predicted = jnp.sum(by_row * along, axis=0, keepdims=True)
        perturbed = line(value_ref) + line(noise_ref)
        for q in range(GATHERED_LINES, count):
            lanes = slice((q - GATHERED_LINES) * LANES, (q - GATHERED_LINES + 1) * LANES)
            put(q, predicted[:, lanes], perturbed[:, lanes])

        for q in range(GATHERED_LINES):
            here = pl.ds(i * count + q, 1)
            place = pl.ds(pl.multiple_of((i * count + q) * LANES, LANES), LANES)

            def spread(value):
                return jnp.broadcast_to(value, (SUBLANES, LANES))

            row = spread(row_ref[here, :])
            first = spread(frac_ref[pl.ds(0, 1), place])
            second = spread(frac_ref[pl.ds(1, 1), place])
            row_other, even_at, odd_at, even_by, odd_by = places(
                row, spread(col_ref[here, :]), spread(quad_ref[here, :]), second
            )
            evens, odds = gather(even_whole_ref, even_at), gather(odd_whole_ref, odd_at)
            total = jnp.zeros((SUBLANES, LANES), jnp.float32)
            for start, even, odd in zip(range(0, rows, SUBLANES), evens, odds):
                by_row = jnp.where(
                    sub == row - start, 1.0 - first, jnp.where(sub == row_other - start, first, 0.0)
                )
                total = total + by_row * (even_by * even + odd_by * odd)
            predicted = jnp.sum(total, axis=0, keepdims=True)
            put(q, predicted, value_ref[here, :] + noise_ref[here, :])
        return carry

    lax.fori_loop(0, row_ref.shape[0] // count, sample, 0)


def forward(tile_count, tile, level_gain, depth, state, low, high, weights, land_mask, obs):
    levels, rows, cols = state.shape
    per = LEVELS_STEP
    packed = (obs[0].shape[0] // (SUBLANES // 2) * PACK_ROWS, LANES)
    smem = pl.BlockSpec(memory_space=pltpu.SMEM)
    vmem = pl.BlockSpec(memory_space=pltpu.VMEM)
    plane = pl.BlockSpec((rows, cols), lambda i: (0, 0))
    halo = pl.BlockSpec((per, 1, cols), lambda i: (i, 0, 0))
    field = pl.BlockSpec((per, rows, cols), lambda i: (i, 0, 0))
    column = pl.pallas_call(
        functools.partial(sum_column, tile_count),
        in_specs=[pl.BlockSpec(memory_space=pl.ANY)] * 6,
        out_specs=vmem,
        out_shape=jax.ShapeDtypeStruct((rows + SUBLANES, cols), jnp.float32),
        scratch_shapes=[
            pltpu.SMEM((levels,), jnp.float32),
            pltpu.SMEM((levels,), jnp.float32),
            pltpu.SMEM((1,), jnp.int32),
            pltpu.VMEM(state.shape, jnp.float32),
            pltpu.VMEM((rows, cols), jnp.float32),
            pltpu.VMEM((rows, cols), jnp.float32),
            pltpu.VMEM((rows, cols), jnp.int32),
            pltpu.SemaphoreType.DMA((levels // per + 5,)),
        ],
        compiler_params=pltpu.CompilerParams(vmem_limit_bytes=VMEM_BYTES),
        cost_estimate=pl.CostEstimate(
            flops=6 * state.size, bytes_accessed=4 * state.size, transcendentals=0
        ),
        name="sum_column",
    )(level_gain, depth, state, weights, land_mask, tile)
    table = pltpu.VMEM((2 * rows * cols // (2 * KEYS), KEYS), jnp.bfloat16)
    sampled = pl.pallas_call(
        sample_column,
        in_specs=[vmem] * (5 + len(obs)),
        out_specs=vmem,
        out_shape=jax.ShapeDtypeStruct(packed, jnp.float32),
        scratch_shapes=[table, table] + [pltpu.VMEM((rows, cols // 2), jnp.float32)] * 2,
        compiler_params=pltpu.CompilerParams(vmem_limit_bytes=MIDDLE_VMEM_BYTES),
        name="sample_column",
    )(column, low, high, weights, land_mask, *obs)
    stepped, mark = pl.pallas_call(
        functools.partial(step_levels, tile_count),
        grid=(levels // per,),
        in_specs=[smem, smem, field, halo, halo, plane, plane, pl.BlockSpec(memory_space=pl.ANY)],
        out_specs=[field, pl.BlockSpec((SUBLANES, LANES), lambda i: (0, 0))],
        out_shape=[
            jax.ShapeDtypeStruct(state.shape, jnp.float32),
            jax.ShapeDtypeStruct((SUBLANES, LANES), jnp.float32),
        ],
        scratch_shapes=[pltpu.VMEM((rows, cols), jnp.float32)],
        compiler_params=pltpu.CompilerParams(vmem_limit_bytes=MIDDLE_VMEM_BYTES),
        cost_estimate=pl.CostEstimate(
            flops=10 * state.size, bytes_accessed=8 * state.size, transcendentals=0
        ),
        name="step_levels",
    )(tile, level_gain, state, low, high, weights, land_mask, sampled)
    return stepped, mark, sampled


def shard_products(index_ref, grouped_ref, error_ref, after_ref, misfit_ref, products_ref):
    del after_ref
    members = misfit_ref.shape[0]
    half_rows = SUBLANES // 2

    def lines(first):
        return jnp.concatenate(
            [grouped_ref[pl.ds(first + q, members, stride=PACK_ROWS), :] for q in range(half_rows)],
            axis=1,
        )

    grouped, misfit = lines(0), lines(half_rows)
    misfit_ref[...] = misfit
    error = jnp.concatenate(
        [error_ref[pl.ds(index_ref[0] * half_rows + q, 1), :] for q in range(half_rows)], axis=1
    )
    anomaly = grouped - jnp.sum(grouped, axis=0, keepdims=True) * (1.0 / members)
    weighted = anomaly / error
    blank = jnp.zeros((LANES - 2 * members, grouped.shape[1]), jnp.float32)
    products = lax.dot_general(
        weighted,
        jnp.concatenate([misfit, anomaly, blank], axis=0),
        (((1,), (1,)), ((), ())),
        precision=lax.Precision.HIGHEST,
        preferred_element_type=jnp.float32,
    )
    half = members // 2
    packed = jnp.concatenate(
        [products[:half, : 2 * members], products[half:, : 2 * members]], axis=1
    )
    for receiver in range(products_ref.shape[0] // half):
        products_ref[pl.ds(receiver * half, half), :] = packed


def total_of(ref, rows):
    total = ref[pl.ds(0, rows), :]
    for sender in range(1, ref.shape[0] // rows):
        total = total + ref[pl.ds(sender * rows, rows), :]
    return total


def sum_and_spread(rows, parts_ref, out_ref):
    total = total_of(parts_ref, rows)
    for receiver in range(out_ref.shape[0] // rows):
        out_ref[pl.ds(receiver * rows, rows), :] = total


def solve_and_combine(total_obs, parts_ref, grouped_ref, out_ref):
    piece = PACK_ROWS - SUBLANES
    members = out_ref.shape[0] // piece
    packed = total_of(parts_ref, members // 2)
    row = lax.broadcasted_iota(jnp.int32, (members, 2 * members), 0)
    lane = lax.broadcasted_iota(jnp.int32, (members, 2 * members), 1)
    system = jnp.concatenate([packed[:, : 2 * members], packed[:, 2 * members :]], axis=0)
    system = system / total_obs + jnp.where(row + members == lane, 1.0, 0.0)
    def pair(a, b, c, d):
        scale = 1.0 / (a * d - b * c)
        return lambda u, v: ((d * u - b * v) * scale, (a * v - c * u) * scale)

    for k in range(0, members, 4):
        spread = [
            jnp.broadcast_to(system[:, at : at + 1], system.shape)
            for at in range(members + k, members + k + 4)
        ]
        m = [[column[k + i : k + i + 1, :] for column in spread] for i in range(4)]
        r = [system[k + i : k + i + 1, :] for i in range(4)]
        solved = pair(m[0][0], m[0][1], m[1][0], m[1][1])
        p0, p1 = solved(r[0], r[1])
        (x0, x1), (y0, y1) = solved(m[0][2], m[1][2]), solved(m[0][3], m[1][3])
        r2, r3 = (r[i] - m[i][0] * p0 - m[i][1] * p1 for i in (2, 3))
        a, c = (m[i][2] - m[i][0] * x0 - m[i][1] * x1 for i in (2, 3))
        b, d = (m[i][3] - m[i][0] * y0 - m[i][1] * y1 for i in (2, 3))
        p2, p3 = pair(a, b, c, d)(r2, r3)
        pivots = [p0 - x0 * p2 - y0 * p3, p1 - x1 * p2 - y1 * p3, p2, p3]
        others = system
        for column, pivot in zip(spread, pivots):
            others = others - column * pivot
        for i, pivot in enumerate(pivots):
            others = jnp.where(row == k + i, pivot, others)
        system = others
    coefficients = system[:, :members]
    combination = coefficients - jnp.sum(coefficients, axis=0, keepdims=True) * (1.0 / members)
    combination = combination + jnp.where(row == lane, 1.0, 0.0)[:, :members]
    weights = jnp.concatenate(
        [grouped_ref[pl.ds(SUBLANES + s, members, stride=PACK_ROWS), :] for s in range(piece)],
        axis=1,
    )
    combined = lax.dot_general(
        combination,
        weights,
        (((0,), (0,)), ((), ())),
        precision=lax.Precision.HIGHEST,
        preferred_element_type=jnp.float32,
    )
    for s in range(piece):
        out_ref[pl.ds(s, members, stride=piece), :] = combined[:, s * LANES : (s + 1) * LANES]


def local(kernel, name, out_shapes, *args):
    vmem = pl.BlockSpec(memory_space=pltpu.VMEM)
    smem = pl.BlockSpec(memory_space=pltpu.SMEM)
    return pl.pallas_call(
        kernel,
        in_specs=[smem if array.dtype == jnp.int32 else vmem for array in args],
        out_specs=[vmem] * len(out_shapes),
        out_shape=[jax.ShapeDtypeStruct(shape, jnp.float32) for shape in out_shapes],
        compiler_params=pltpu.CompilerParams(vmem_limit_bytes=SMALL_VMEM_BYTES),
        name=name,
    )(*args)


def swap(array, axes):
    count = lax.axis_size(axes)
    pieces = array.reshape(count, array.shape[0] // count, array.shape[1])
    moved = lax.all_to_all(pieces, axes, split_axis=0, concat_axis=0, tiled=True)
    return moved.reshape(array.shape)


def on_device(
    state,
    weights,
    land_mask,
    level_gain,
    depth,
    obs_row,
    obs_col,
    obs_quad,
    obs_frac,
    obs_value,
    obs_error,
    noise,
):
    axes = ("half", "member")
    members = lax.axis_size(axes)
    index = lax.axis_index(axes).astype(jnp.int32).reshape(1)
    tile_count = lax.axis_size("tile")
    obs_local = obs_row.shape[0]
    total_obs = obs_local * tile_count
    own = state[0]
    up = [(i, (i + 1) % tile_count) for i in range(tile_count)]
    down = [(target, source) for source, target in up]
    low = lax.ppermute(own[:, -1:], "tile", up)
    high = lax.ppermute(own[:, :1], "tile", down)
    tile = lax.axis_index("tile").astype(jnp.int32).reshape(1)
    grid = (obs_local // LANES, LANES)
    obs = (
        obs_row.reshape(grid),
        obs_col.reshape(grid),
        obs_quad.reshape(grid),
        obs_frac,
        obs_value.reshape(grid),
        noise.reshape(grid),
    )
    stepped, stepped_mark, sampled = forward(
        tile_count, tile, level_gain, depth, own, low, high, weights[0], land_mask, obs
    )
    grouped = swap(sampled, axes)
    packed_rows = members // 2
    misfit, products = local(
        shard_products,
        "shard_products",
        [(members, obs_local // members), (tile_count * packed_rows, LANES)],
        index,
        grouped,
        obs_error.reshape(grid),
        stepped_mark,
    )
    (products,) = local(
        functools.partial(sum_and_spread, packed_rows),
        "sum_and_spread",
        [(members * packed_rows, LANES)],
        swap(products, "tile"),
    )
    (combined,) = local(
        functools.partial(solve_and_combine, total_obs),
        "solve_and_combine",
        [(members * (PACK_ROWS - SUBLANES), LANES)],
        swap(products, axes),
        grouped,
    )
    tiles = swap(combined, axes)
    _, rows, cols = weights.shape
    new_weights = (
        tiles.reshape(rows // SUBLANES, cols // LANES, SUBLANES, LANES)
        .transpose(0, 2, 1, 3)
        .reshape(weights.shape)
    )
    return (stepped[None], new_weights, misfit)


def solution(mesh):
    in_specs = (
        P(("half", "member"), None, "tile", None),
        P(("half", "member"), "tile", None),
        P("tile", None),
        P(),
        P(),
        P("tile"),
        P("tile"),
        P("tile"),
        P(None, "tile"),
        P("tile"),
        P("tile"),
        P(("half", "member"), "tile"),
    )
    out_specs = (
        P(("half", "member"), None, "tile", None),
        P(("half", "member"), "tile", None),
        P(None, ("half", "member", "tile")),
    )
    return jax.shard_map(
        on_device, mesh=mesh, in_specs=in_specs, out_specs=out_specs, check_vma=False
    )
```
